256 devices in a mesh: row: 16 (over x, z_hi, core), col: 16 (over y, z_lo).
Axes of the slice: x: 4, y: 4, z: 8 (z_hi: 2, z_lo: 4; z = z_hi * 4 + z_lo), core: 2. Of those that a mesh axis runs over, the one named last changes fastest.
Arguments:
- feats_one: bfloat16 [32768, 1536], P(('row', 'col')), may hold values from -4 to 4
- feats_two: bfloat16 [32768, 1536], P(('col', 'row')), may hold values from -4 to 4
- w_first: bfloat16 [1536, 512], replicated, may hold values from -0.15625 to 0.15625
- w_second: bfloat16 [512, 128], replicated, may hold values from -0.25 to 0.25
Outputs:
- mapped: float32 [32768, 128], P(('row', 'col'))
The draws below stay inside these ranges and needn't reach their ends.
All inputs are finite; a program needn't handle non-finite values.
Results may differ from the reference program's by a relative error of at most 0.0022.
Values may be sent and summed in bfloat16 or wider, within the bound.
No kernel may reach another device: no remote copies, remote signals or barrier semaphores. Data moves between devices by JAX's collectives and lax.ppermute only.
A program may use at most 64 MiB of HBM per device.

```python
import jax
import jax.numpy as jnp
from jax import lax

D_IN = 1536
HID = 512
EMB = 128
SWEEPS = 3
BLOCK = 2048
N_ONE = 32768
N_TWO = 32768
N_ROW = 16


def common_curve(key):
    freqs = jax.random.randint(jax.random.fold_in(key, 1), (D_IN,), 1, 6).astype(jnp.float32)
    phases = jax.random.uniform(jax.random.fold_in(key, 2), (D_IN,), jnp.float32)
    return (freqs, phases)


def curve_features(key, count, waves, warp_amount, freqs, phases, noise):
    jitter = jax.random.uniform(jax.random.fold_in(key, 3), (count,), jnp.float32)
    turn = jax.random.uniform(jax.random.fold_in(key, 4), (), jnp.float32)
    place = (jnp.arange(count, dtype=jnp.float32) + 0.5) / count + 0.375 * jitter
    angle = 2.0 * jnp.pi * (waves * place + turn)
    spot = place + warp_amount / (2.0 * jnp.pi * waves) * jnp.sin(angle)
    smooth = jnp.cos(2.0 * jnp.pi * (spot[:, None] * freqs[None, :] + phases[None, :]))
    return jnp.sqrt(1.4) * smooth + jnp.sqrt(0.3) * noise


def draw_feats_one(key, part):
    freqs, phases = common_curve(key)
    key = jax.random.fold_in(key, 11)
    noise_key = jax.random.fold_in(key, 5)
    noise = jnp.clip(jax.random.normal(noise_key, (N_ONE, D_IN), jnp.float32), -5.0, 5.0)
    return curve_features(key, N_ONE, 2.0, 0.6, freqs, phases, noise).astype(jnp.bfloat16)


def draw_feats_two(key, part):
    freqs, phases = common_curve(key)
    key = jax.random.fold_in(key, 23)
    noise_key = jax.random.fold_in(key, 5)
    noise = jnp.clip(jax.random.normal(noise_key, (N_TWO, D_IN), jnp.float32), -5.0, 5.0)
    return curve_features(key, N_TWO, 3.0, 0.6, freqs, phases, noise).astype(jnp.bfloat16)


def normal_values(own_key, extent, deviation, bound, kind=jnp.bfloat16):
    drawn = jax.random.normal(own_key, extent, jnp.float32) * deviation
    return jnp.minimum(jnp.maximum(drawn, -bound), bound).astype(kind)


def setup_inputs(seed: int = 0) -> dict:
    key_of = jax.random.split(jax.random.key(seed), 5)
    feats_one = draw_feats_one(jax.random.fold_in(key_of[4], 71), 0)
    feats_two = draw_feats_two(jax.random.fold_in(key_of[4], 71), 0)
    w_first = normal_values(key_of[2], (D_IN, HID), D_IN ** -0.5, 0.15625)
    w_second = normal_values(key_of[3], (HID, EMB), HID ** -0.5, 0.25)
    return {"feats_one": feats_one, "feats_two": feats_two, "w_first": w_first, "w_second": w_second}


def embed(feats, w_first, w_second):
    hidden = jax.nn.relu(jnp.dot(feats, w_first, preferred_element_type=jnp.float32)).astype(jnp.bfloat16)
    plain = jnp.dot(hidden, w_second, preferred_element_type=jnp.float32).astype(jnp.bfloat16)
    wide = plain.astype(jnp.float32)
    unit = (wide / jnp.sqrt(lax.optimization_barrier(jnp.sum(wide * wide, axis=1, keepdims=True)) + 1e-06)).astype(jnp.bfloat16)
    return (plain, unit)

def reference(feats_one, feats_two, w_first, w_second):
    plain_one, unit_one = embed(feats_one, w_first, w_second)
    plain_two, unit_two = embed(feats_two, w_first, w_second)
    blocks = unit_one.reshape(N_ROW, BLOCK, EMB)
    kernel = lax.map(lambda blk: jnp.exp(20.0 * jnp.dot(blk, unit_two.T, preferred_element_type=jnp.float32)), blocks)
    col_scale = jnp.ones((N_TWO,), jnp.float32)
    row_scale = jnp.ones((N_ROW, BLOCK), jnp.float32)
    for sweep in range(SWEEPS):
        sums = lax.map(lambda kblk: jnp.dot(kblk, col_scale, precision=lax.Precision.HIGHEST), kernel)
        row_scale = 1.0 / sums
        col_sums = jnp.einsum('brc,br->c', kernel, row_scale, precision=lax.Precision.HIGHEST)
        col_scale = 1.0 / col_sums

    def transport(pair):
        kblk, ublk = pair
        scaled = (kblk * col_scale[None, :]).astype(jnp.bfloat16)
        return ublk[:, None] * jnp.dot(scaled, plain_two, preferred_element_type=jnp.float32)
    mapped = lax.map(transport, (kernel, row_scale))
    return mapped.reshape(N_ONE, EMB)
```

```python
import math

import jax
import jax.numpy as jnp
from jax import lax
from jax.experimental import pallas as pl
from jax.experimental.pallas import tpu as pltpu
from jax.sharding import Mesh
from jax.sharding import PartitionSpec as P

SWEEPS = 3
PEERS = 16
LANES = 128
SIDE = PEERS * LANES
EXPONENT = 20.0 * math.log2(math.e)
AXES = ("xh", "xl", "zh", "c", "yh", "yl", "zm", "zl")
SAME_ROWS = ("xh", "xl", "yl", "c")
SAME_COLS = ("yh", "zh", "zm", "zl")
F32, BF16 = jnp.float32, jnp.bfloat16
VMEM_LIMIT = 40 * 2**20


def unit_of(plain):
    wide = plain.astype(F32)
    return (wide / jnp.sqrt(jnp.sum(wide * wide, axis=1, keepdims=True) + 1e-06)).astype(BF16)


def embed_kernel(one_ref, two_ref, first_ref, second_ref, unit_ref, plain_ref):
    feats = jnp.concatenate([one_ref[...], two_ref[...]], axis=0)
    hidden = jnp.maximum(jnp.dot(feats, first_ref[...], preferred_element_type=F32), 0.0).astype(BF16)
    plain = jnp.dot(hidden, second_ref[...], preferred_element_type=F32).astype(BF16)
    unit = unit_of(plain[:LANES])
    for peer in range(PEERS):
        unit_ref[peer] = unit
        plain_ref[peer] = plain[LANES:]


def row_totals(parts):
    return jnp.sum(parts.T, axis=0, keepdims=True)


def fill(out_ref, lines_ref):
    lines = lines_ref[...]
    for peer in range(PEERS):
        out_ref[peer] = lines


def tile_kernel(left_ref, plain_ref, tile_ref, sums_ref, units_ref, lines_ref):
    units_ref[...] = unit_of(plain_ref[...].reshape(SIDE, LANES))

    @pl.loop(0, PEERS // 2)
    def _(step):
        left = left_ref[pl.ds(2 * step, 2)].reshape(2 * LANES, LANES)
        rows = pl.ds(pl.multiple_of(step * 2 * LANES, 2 * LANES), 2 * LANES)
        parts = jnp.zeros((2 * LANES, LANES), F32)
        for chunk in range(PEERS // 2):
            right = units_ref[chunk * 2 * LANES : (chunk + 1) * 2 * LANES]
            dots = lax.dot_general(left, right, (((1,), (1,)), ((), ())), preferred_element_type=F32)
            block = jnp.exp2(dots * EXPONENT)
            tile_ref[rows, chunk * 2 * LANES : (chunk + 1) * 2 * LANES] = block
            parts += block[:, :LANES] + block[:, LANES:]
        lines_ref[pl.ds(2 * step, 1)] = row_totals(parts[:LANES])
        lines_ref[pl.ds(2 * step + 1, 1)] = row_totals(parts[LANES:])

    fill(sums_ref, lines_ref)


def scale_of(got_ref):
    total = got_ref[0]
    for peer in range(1, PEERS):
        total += got_ref[peer]
    return 1.0 / total


def cols_kernel(got_ref, tile_ref, sums_ref, scale_ref, lines_ref):
    scale_ref[...] = scale_of(got_ref)
    zero = tuple(jnp.zeros((8, LANES), F32) for _ in range(PEERS))

    def step(block, parts):
        rows = pl.ds(pl.multiple_of(block * LANES, LANES), LANES)
        factor = jnp.broadcast_to(scale_ref[pl.ds(block, 1)], (LANES, LANES)).T
        out = []
        for chunk in range(PEERS):
            product = tile_ref[rows, chunk * LANES : (chunk + 1) * LANES] * factor
            out.append(parts[chunk] + jnp.sum(product.reshape(LANES // 8, 8, LANES), axis=0))
        return tuple(out)

    parts = lax.fori_loop(0, PEERS, step, zero)
    for chunk in range(PEERS):
        lines_ref[chunk : chunk + 1] = jnp.sum(parts[chunk], axis=0, keepdims=True)
    fill(sums_ref, lines_ref)


def rows_kernel(got_ref, tile_ref, sums_ref, lines_ref):
    scale = scale_of(got_ref)

    @pl.loop(0, PEERS)
    def _(block):
        rows = pl.ds(pl.multiple_of(block * LANES, LANES), LANES)
        parts = tile_ref[rows, :LANES] * scale[:1]
        for chunk in range(1, PEERS):
            parts += tile_ref[rows, chunk * LANES : (chunk + 1) * LANES] * scale[chunk : chunk + 1]
        lines_ref[pl.ds(block, 1)] = row_totals(parts)

    fill(sums_ref, lines_ref)


def map_kernel(got_ref, tile_ref, plain_ref, out_ref):
    scale = scale_of(got_ref)
    wide = jnp.concatenate([scale[chunk : chunk + 1] for chunk in range(PEERS)], axis=1)
    plain = plain_ref[...].reshape(SIDE, LANES)

    @pl.loop(0, PEERS // 2)
    def _(step):
        rows = pl.ds(pl.multiple_of(step * 2 * LANES, 2 * LANES), 2 * LANES)
        scaled = (tile_ref[rows, :] * wide).astype(BF16)
        part = jnp.dot(scaled, plain, preferred_element_type=F32)
        out_ref[pl.ds(2 * step, 2)] = part.reshape(2, LANES, LANES)


def finish_kernel(got_ref, scale_ref, out_ref):
    total = got_ref[0].astype(F32)
    for peer in range(1, PEERS):
        total += got_ref[peer].astype(F32)
    out_ref[...] = total * jnp.broadcast_to(scale_ref[...], (LANES, LANES)).T


def call(kernel, outs, *args, scratch=(), flops=0, exps=0):
    moved = sum(math.prod(a.shape) * a.dtype.itemsize for a in args)
    return pl.pallas_call(
        kernel,
        out_shape=outs,
        scratch_shapes=scratch,
        compiler_params=pltpu.CompilerParams(vmem_limit_bytes=VMEM_LIMIT),
        cost_estimate=pl.CostEstimate(flops=flops, bytes_accessed=moved, transcendentals=exps),
    )(*args)


def near(array):
    return pltpu.with_memory_space_constraint(array, pltpu.VMEM)


def exchange(array, axes):
    return lax.all_to_all(array, axes, 0, 0)


def on_device(feats_one, feats_two, w_first, w_second):
    spread = jax.ShapeDtypeStruct((PEERS, LANES, LANES), BF16)
    vectors = jax.ShapeDtypeStruct((PEERS, PEERS, LANES), F32)
    lines = pltpu.VMEM((PEERS, LANES), F32)
    unit_one, plain_two = call(embed_kernel, (spread, spread), feats_one, feats_two, w_first, w_second)
    plains = exchange(plain_two, SAME_COLS)
    units = exchange(unit_one, SAME_ROWS)
    tile, sums = call(
        tile_kernel,
        (pltpu.VMEM((SIDE, SIDE), F32), vectors),
        units,
        plains,
        scratch=(pltpu.VMEM((SIDE, LANES), BF16), lines),
    )
    tile = near(tile)
    for sweep in range(SWEEPS):
        if sweep:
            sums = call(rows_kernel, vectors, sums, tile, scratch=(lines,))
        sums = exchange(sums, SAME_ROWS)
        sums, row_scale = call(
            cols_kernel,
            (vectors, jax.ShapeDtypeStruct((PEERS, LANES), F32)),
            sums,
            tile,
            scratch=(lines,),
        )
        sums = exchange(sums, SAME_COLS)
    parts = call(map_kernel, jax.ShapeDtypeStruct((PEERS, LANES, LANES), F32), sums, tile, plains)
    parts = exchange(parts, SAME_ROWS)
    own = lax.dynamic_slice_in_dim(row_scale, lax.axis_index(SAME_ROWS), 1, 0)
    return call(finish_kernel, jax.ShapeDtypeStruct((LANES, LANES), F32), parts, own)


def solution(mesh):
    fine = Mesh(mesh.devices.reshape((2,) * 8), AXES)
    row, col = AXES[:4], AXES[4:]
    return jax.shard_map(
        on_device,
        mesh=fine,
        in_specs=(P(row + col, None), P(col + row, None), P(), P()),
        out_specs=P(row + col, None),
        check_vma=False,
    )
```

```python
import math

import jax
import jax.numpy as jnp
from jax import lax
from jax.experimental import pallas as pl
from jax.experimental.pallas import tpu as pltpu
from jax.sharding import Mesh
from jax.sharding import PartitionSpec as P

SWEEPS = 3
PEERS = 16
LANES = 128
SIDE = PEERS * LANES
EXPONENT = 20.0 * math.log2(math.e)
AXES = ("xh", "xl", "zh", "c", "yh", "yl", "zm", "zl")
SAME_ROWS = ("xh", "xl", "yh", "yl")
SAME_COLS = ("zh", "zm", "zl", "c")
F32, BF16 = jnp.float32, jnp.bfloat16
VMEM_LIMIT = 16 * 2**20


def unit_of(plain):
    wide = plain.astype(F32)
    return (wide / jnp.sqrt(jnp.sum(wide * wide, axis=1, keepdims=True) + 1e-06)).astype(BF16)


def embed_kernel(one_hbm, two_hbm, first_hbm, second_hbm, unit_ref, plain_ref, feats_ref, first_ref, second_ref, sems):
    copies = [
        pltpu.make_async_copy(first_hbm, first_ref, sems.at[0]),
        pltpu.make_async_copy(one_hbm, feats_ref.at[pl.ds(0, LANES)], sems.at[1]),
        pltpu.make_async_copy(two_hbm, feats_ref.at[pl.ds(LANES, LANES)], sems.at[2]),
        pltpu.make_async_copy(second_hbm, second_ref, sems.at[3]),
    ]
    for copy in copies:
        copy.start()
    for copy in copies:
        copy.wait()
    hidden = jnp.dot(feats_ref[...], first_ref[...], preferred_element_type=F32)
    hidden = jnp.maximum(hidden, 0.0).astype(BF16)
    plain = jnp.dot(hidden, second_ref[...], preferred_element_type=F32).astype(BF16)
    unit = unit_of(plain[:LANES])
    for peer in range(PEERS):
        unit_ref[peer] = unit
        plain_ref[peer] = plain[LANES:]


def row_totals(parts):
    return jnp.sum(parts.T, axis=0, keepdims=True)


def fill(out_ref, lines_ref):
    lines = lines_ref[...]
    for peer in range(PEERS):
        out_ref[peer] = lines


def tile_kernel(left_ref, plain_ref, tile_ref, sums_ref, units_ref, lines_ref):
    units_ref[...] = unit_of(plain_ref[...].reshape(SIDE, LANES))

    @pl.loop(0, PEERS // 2)
    def _(step):
        left = left_ref[pl.ds(2 * step, 2)].reshape(2 * LANES, LANES)
        rows = pl.ds(pl.multiple_of(step * 2 * LANES, 2 * LANES), 2 * LANES)
        parts = jnp.zeros((2 * LANES, LANES), F32)
        for chunk in range(PEERS // 2):
            right = units_ref[chunk * 2 * LANES : (chunk + 1) * 2 * LANES]
            dots = lax.dot_general(left, right, (((1,), (1,)), ((), ())), preferred_element_type=F32)
            block = jnp.exp2(dots * EXPONENT)
            tile_ref[rows, chunk * 2 * LANES : (chunk + 1) * 2 * LANES] = block
            parts += block[:, :LANES] + block[:, LANES:]
        lines_ref[pl.ds(2 * step, 1)] = row_totals(parts[:LANES])
        lines_ref[pl.ds(2 * step + 1, 1)] = row_totals(parts[LANES:])

    fill(sums_ref, lines_ref)


def scale_of(got_ref):
    total = got_ref[0]
    for peer in range(1, PEERS):
        total += got_ref[peer]
    return 1.0 / total


def cols_kernel(got_ref, tile_ref, sums_ref, scale_ref, lines_ref):
    scale_ref[...] = scale_of(got_ref)
    zero = tuple(jnp.zeros((8, LANES), F32) for _ in range(PEERS))

    def step(block, parts):
        rows = pl.ds(pl.multiple_of(block * LANES, LANES), LANES)
        factor = jnp.broadcast_to(scale_ref[pl.ds(block, 1)], (LANES, LANES)).T
        out = []
        for chunk in range(PEERS):
            product = tile_ref[rows, chunk * LANES : (chunk + 1) * LANES] * factor
            out.append(parts[chunk] + jnp.sum(product.reshape(LANES // 8, 8, LANES), axis=0))
        return tuple(out)

    parts = lax.fori_loop(0, PEERS, step, zero)
    for chunk in range(PEERS):
        lines_ref[chunk : chunk + 1] = jnp.sum(parts[chunk], axis=0, keepdims=True)
    fill(sums_ref, lines_ref)


def rows_kernel(got_ref, tile_ref, sums_ref, lines_ref):
    scale = scale_of(got_ref)

    @pl.loop(0, PEERS)
    def _(block):
        rows = pl.ds(pl.multiple_of(block * LANES, LANES), LANES)
        parts = tile_ref[rows, :LANES] * scale[:1]
        for chunk in range(1, PEERS):
            parts += tile_ref[rows, chunk * LANES : (chunk + 1) * LANES] * scale[chunk : chunk + 1]
        lines_ref[pl.ds(block, 1)] = row_totals(parts)

    fill(sums_ref, lines_ref)


def map_kernel(got_ref, tile_ref, plain_ref, out_ref):
    scale = scale_of(got_ref)
    wide = jnp.concatenate([scale[chunk : chunk + 1] for chunk in range(PEERS)], axis=1)
    plain = plain_ref[...].reshape(SIDE, LANES)

    @pl.loop(0, PEERS // 2)
    def _(step):
        rows = pl.ds(pl.multiple_of(step * 2 * LANES, 2 * LANES), 2 * LANES)
        scaled = (tile_ref[rows, :] * wide).astype(BF16)
        part = jnp.dot(scaled, plain, preferred_element_type=F32)
        out_ref[pl.ds(2 * step, 2)] = part.reshape(2, LANES, LANES)


def finish_kernel(got_ref, scale_ref, out_ref):
    total = got_ref[0].astype(F32)
    for peer in range(1, PEERS):
        total += got_ref[peer].astype(F32)
    out_ref[...] = total * jnp.broadcast_to(scale_ref[...], (LANES, LANES)).T


def call(kernel, outs, *args, scratch=(), flops=0, exps=0, limit=VMEM_LIMIT, **specs):
    moved = sum(math.prod(a.shape) * a.dtype.itemsize for a in args)
    return pl.pallas_call(
        kernel,
        out_shape=outs,
        **specs,
        scratch_shapes=scratch,
        compiler_params=pltpu.CompilerParams(vmem_limit_bytes=limit),
        cost_estimate=pl.CostEstimate(flops=flops, bytes_accessed=moved, transcendentals=exps),
    )(*args)


def near(array):
    return pltpu.with_memory_space_constraint(array, pltpu.VMEM)


def exchange(array, axes):
    return lax.all_to_all(array, axes, 0, 0)


def on_device(feats_one, feats_two, w_first, w_second):
    spread = pltpu.VMEM((PEERS, LANES, LANES), BF16)
    vectors = pltpu.VMEM((PEERS, PEERS, LANES), F32)
    lines = pltpu.VMEM((PEERS, LANES), F32)
    rows = feats_one.shape[0] + feats_two.shape[0]
    unit_one, plain_two = call(
        embed_kernel,
        (spread, spread),
        feats_one,
        feats_two,
        w_first,
        w_second,
        in_specs=[pl.BlockSpec(memory_space=pltpu.HBM)] * 4,
        limit=60 * 2**20,
        scratch=(
            pltpu.VMEM((rows, feats_one.shape[1]), BF16),
            pltpu.VMEM(w_first.shape, BF16),
            pltpu.VMEM(w_second.shape, BF16),
            pltpu.SemaphoreType.DMA((4,)),
        ),
    )
    plains = near(exchange(plain_two, SAME_COLS))
    units = near(exchange(unit_one, SAME_ROWS))
    tile, sums = call(
        tile_kernel,
        (pltpu.VMEM((SIDE, SIDE), F32), vectors),
        units,
        plains,
        scratch=(pltpu.VMEM((SIDE, LANES), BF16), lines),
    )
    tile = near(tile)
    for sweep in range(SWEEPS):
        if sweep:
            sums = call(rows_kernel, vectors, sums, tile, scratch=(lines,))
        sums = near(exchange(sums, SAME_ROWS))
        sums, row_scale = call(cols_kernel, (vectors, lines), sums, tile, scratch=(lines,))
        sums = near(exchange(sums, SAME_COLS))
    parts = call(map_kernel, pltpu.VMEM((PEERS, LANES, LANES), F32), sums, tile, plains)
    parts = near(exchange(parts, SAME_ROWS))
    own = lax.dynamic_slice_in_dim(row_scale, lax.axis_index(SAME_ROWS), 1, 0)
    return call(finish_kernel, jax.ShapeDtypeStruct((LANES, LANES), F32), parts, own)


def solution(mesh):
    fine = Mesh(mesh.devices.reshape((2,) * 8), AXES)
    row, col = AXES[:4], AXES[4:]
    return jax.shard_map(
        on_device,
        mesh=fine,
        in_specs=(P(row + col, None), P(col + row, None), P(), P()),
        out_specs=P(row + col, None),
        check_vma=False,
    )
```

```python
import math

import jax
import jax.numpy as jnp
from jax import lax
from jax.experimental import pallas as pl
from jax.experimental.pallas import tpu as pltpu
from jax.sharding import Mesh
from jax.sharding import PartitionSpec as P

SWEEPS = 3
PEERS = 16
LANES = 128
SIDE = PEERS * LANES
EXPONENT = 20.0 * math.log2(math.e)
AXES = ("xh", "xl", "zh", "c", "yh", "yl", "zm", "zl")
SAME_ROWS = ("xh", "xl", "yh", "yl")
SAME_COLS = ("zh", "zm", "zl", "c")
RING = SAME_COLS[:3]
HALF = SIDE // 2
SWAP = [(0, 1), (1, 0)]
F32, BF16 = jnp.float32, jnp.bfloat16
VMEM_LIMIT = 16 * 2**20


def unit_of(plain):
    wide = plain.astype(F32)
    return (wide / jnp.sqrt(jnp.sum(wide * wide, axis=1, keepdims=True) + 1e-06)).astype(BF16)


def embed_kernel(one_hbm, two_hbm, first_hbm, second_hbm, unit_ref, plain_ref, feats_ref, first_ref, second_ref, sems):
    copies = [
        pltpu.make_async_copy(first_hbm, first_ref, sems.at[0]),
        pltpu.make_async_copy(one_hbm, feats_ref.at[pl.ds(0, LANES)], sems.at[1]),
        pltpu.make_async_copy(two_hbm, feats_ref.at[pl.ds(LANES, LANES)], sems.at[2]),
        pltpu.make_async_copy(second_hbm, second_ref, sems.at[3]),
    ]
    for copy in copies:
        copy.start()
    for copy in copies:
        copy.wait()
    hidden = jnp.dot(feats_ref[...], first_ref[...], preferred_element_type=F32)
    hidden = jnp.maximum(hidden, 0.0).astype(BF16)
    plain = jnp.dot(hidden, second_ref[...], preferred_element_type=F32).astype(BF16)
    unit = unit_of(plain[:LANES])
    for peer in range(PEERS):
        unit_ref[peer] = unit
    for peer in range(PEERS // 2):
        plain_ref[peer] = plain[LANES:]


def row_totals(parts):
    return jnp.sum(parts.T, axis=0, keepdims=True)


def fill(out_ref, lines_ref):
    lines = lines_ref[...]
    for peer in range(PEERS):
        out_ref[peer] = lines


def tile_kernel(left_ref, mine_ref, other_ref, tile_ref, sums_ref, plain_ref, units_ref, lines_ref):
    core = lax.axis_index("c")
    for half, got_ref in ((core, mine_ref), (1 - core, other_ref)):
        place = pl.ds(pl.multiple_of(half * HALF, HALF), HALF)
        plain = got_ref[...].reshape(HALF, LANES)
        plain_ref[place, :] = plain
        units_ref[place, :] = unit_of(plain)

    @pl.loop(0, PEERS // 2)
    def _(step):
        left = left_ref[pl.ds(2 * step, 2)].reshape(2 * LANES, LANES)
        rows = pl.ds(pl.multiple_of(step * 2 * LANES, 2 * LANES), 2 * LANES)
        parts = jnp.zeros((2 * LANES, LANES), F32)
        for chunk in range(PEERS // 2):
            right = units_ref[chunk * 2 * LANES : (chunk + 1) * 2 * LANES]
            dots = lax.dot_general(left, right, (((1,), (1,)), ((), ())), preferred_element_type=F32)
            block = jnp.exp2(dots * EXPONENT)
            tile_ref[rows, chunk * 2 * LANES : (chunk + 1) * 2 * LANES] = block
            parts += block[:, :LANES] + block[:, LANES:]
        lines_ref[pl.ds(2 * step, 1)] = row_totals(parts[:LANES])
        lines_ref[pl.ds(2 * step + 1, 1)] = row_totals(parts[LANES:])

    fill(sums_ref, lines_ref)


def scale_of(got_ref):
    total = got_ref[0]
    for peer in range(1, PEERS):
        total += got_ref[peer]
    return 1.0 / total


def cols_kernel(got_ref, tile_ref, sums_ref, scale_ref, lines_ref):
    scale_ref[...] = scale_of(got_ref)
    zero = tuple(jnp.zeros((8, LANES), F32) for _ in range(PEERS))

    def step(block, parts):
        rows = pl.ds(pl.multiple_of(block * LANES, LANES), LANES)
        factor = jnp.broadcast_to(scale_ref[pl.ds(block, 1)], (LANES, LANES)).T
        out = []
        for chunk in range(PEERS):
            product = tile_ref[rows, chunk * LANES : (chunk + 1) * LANES] * factor
            out.append(parts[chunk] + jnp.sum(product.reshape(LANES // 8, 8, LANES), axis=0))
        return tuple(out)

    parts = lax.fori_loop(0, PEERS, step, zero)
    for chunk in range(PEERS):
        lines_ref[chunk : chunk + 1] = jnp.sum(parts[chunk], axis=0, keepdims=True)
    fill(sums_ref, lines_ref)


def rows_kernel(got_ref, tile_ref, sums_ref, lines_ref):
    scale = scale_of(got_ref)

    @pl.loop(0, PEERS)
    def _(block):
        rows = pl.ds(pl.multiple_of(block * LANES, LANES), LANES)
        parts = tile_ref[rows, :LANES] * scale[:1]
        for chunk in range(1, PEERS):
            parts += tile_ref[rows, chunk * LANES : (chunk + 1) * LANES] * scale[chunk : chunk + 1]
        lines_ref[pl.ds(block, 1)] = row_totals(parts)

    fill(sums_ref, lines_ref)


def map_kernel(got_ref, tile_ref, plain_ref, out_ref):
    scale = scale_of(got_ref)
    wide = jnp.concatenate([scale[chunk : chunk + 1] for chunk in range(PEERS)], axis=1)
    plain = plain_ref[...]

    @pl.loop(0, PEERS // 2)
    def _(step):
        rows = pl.ds(pl.multiple_of(step * 2 * LANES, 2 * LANES), 2 * LANES)
        scaled = (tile_ref[rows, :] * wide).astype(BF16)
        part = jnp.dot(scaled, plain, preferred_element_type=F32)
        out_ref[pl.ds(2 * step, 2)] = part.reshape(2, LANES, LANES).astype(BF16)


def finish_kernel(got_ref, scale_ref, out_ref):
    total = got_ref[0].astype(F32)
    for peer in range(1, PEERS):
        total += got_ref[peer].astype(F32)
    scale = scale_ref[pl.ds(lax.axis_index(SAME_ROWS), 1)]
    out_ref[...] = total * jnp.broadcast_to(scale, (LANES, LANES)).T


def call(kernel, outs, *args, scratch=(), flops=0, exps=0, limit=VMEM_LIMIT, **specs):
    moved = sum(math.prod(a.shape) * a.dtype.itemsize for a in args)
    return pl.pallas_call(
        kernel,
        out_shape=outs,
        **specs,
        scratch_shapes=scratch,
        compiler_params=pltpu.CompilerParams(vmem_limit_bytes=limit),
        cost_estimate=pl.CostEstimate(flops=flops, bytes_accessed=moved, transcendentals=exps),
    )(*args)


def near(array):
    return pltpu.with_memory_space_constraint(array, pltpu.VMEM)


def exchange(array, axes):
    return lax.all_to_all(array, axes, 0, 0)


def on_device(feats_one, feats_two, w_first, w_second):
    spread = pltpu.VMEM((PEERS, LANES, LANES), BF16)
    vectors = pltpu.VMEM((PEERS, PEERS, LANES), F32)
    lines = pltpu.VMEM((PEERS, LANES), F32)
    rows = feats_one.shape[0] + feats_two.shape[0]
    unit_one, plain_two = call(
        embed_kernel,
        (spread, pltpu.VMEM((PEERS // 2, LANES, LANES), BF16)),
        feats_one,
        feats_two,
        w_first,
        w_second,
        in_specs=[pl.BlockSpec(memory_space=pltpu.HBM)] * 4,
        limit=60 * 2**20,
        scratch=(
            pltpu.VMEM((rows, feats_one.shape[1]), BF16),
            pltpu.VMEM(w_first.shape, BF16),
            pltpu.VMEM(w_second.shape, BF16),
            pltpu.SemaphoreType.DMA((4,)),
        ),
    )
    mine = exchange(plain_two, RING)
    other = lax.ppermute(mine, "c", SWAP)
    mine, unit_one = lax.optimization_barrier((mine, unit_one))
    units = exchange(unit_one, SAME_ROWS)
    tile, sums, plains = call(
        tile_kernel,
        (pltpu.VMEM((SIDE, SIDE), F32), vectors, pltpu.VMEM((SIDE, LANES), BF16)),
        near(units),
        near(mine),
        near(other),
        scratch=(pltpu.VMEM((SIDE, LANES), BF16), lines),
    )
    tile = near(tile)
    for sweep in range(SWEEPS):
        if sweep:
            sums = call(rows_kernel, vectors, sums, tile, scratch=(lines,))
        sums = near(exchange(sums, SAME_ROWS))
        sums, row_scale = call(cols_kernel, (vectors, lines), sums, tile, scratch=(lines,))
        sums = near(exchange(sums, SAME_COLS))
    parts = call(map_kernel, spread, sums, tile, near(plains))
    parts = near(exchange(parts, SAME_ROWS))
    return call(finish_kernel, jax.ShapeDtypeStruct((LANES, LANES), F32), parts, row_scale)


def solution(mesh):
    fine = Mesh(mesh.devices.reshape((2,) * 8), AXES)
    row, col = AXES[:4], AXES[4:]
    return jax.shard_map(
        on_device,
        mesh=fine,
        in_specs=(P(row + col, None), P(col + row, None), P(), P()),
        out_specs=P(row + col, None),
        check_vma=False,
    )
```

```python
import functools
import math

import jax
import jax.numpy as jnp
from jax import lax
from jax.experimental import pallas as pl
from jax.experimental.pallas import tpu as pltpu
from jax.sharding import Mesh
from jax.sharding import PartitionSpec as P

SWEEPS = 3
PIECES = 3
PEERS = 16
LANES = 128
SIDE = PEERS * LANES
EXPONENT = 20.0 * math.log2(math.e)
AXES = ("xh", "xl", "zh", "c", "yh", "yl", "zm", "zl")
SAME_ROWS = ("xh", "xl", "yh", "yl")
SAME_COLS = ("zh", "zm", "zl", "c")
RING = SAME_COLS[:3]
HALF = SIDE // 2
SWAP = [(0, 1), (1, 0)]
F32, BF16 = jnp.float32, jnp.bfloat16
VMEM_LIMIT = 16 * 2**20


def unit_of(plain):
    wide = plain.astype(F32)
    return (wide / jnp.sqrt(jnp.sum(wide * wide, axis=1, keepdims=True) + 1e-06)).astype(BF16)


def embed_kernel(feats_hbm, first_hbm, second_hbm, out_ref, feats_ref, first_ref, second_ref, sems, *, unit):
    depth = first_hbm.shape[0] // PIECES
    copies = [pltpu.make_async_copy(feats_hbm, feats_ref, sems.at[PIECES])]
    for piece in range(PIECES):
        place = pl.ds(piece * depth, depth)
        copies.append(pltpu.make_async_copy(first_hbm.at[place], first_ref.at[place], sems.at[piece]))
    copies.append(pltpu.make_async_copy(second_hbm, second_ref, sems.at[PIECES + 1]))
    for copy in copies:
        copy.start()
    copies[0].wait()
    hidden = jnp.zeros((LANES, first_hbm.shape[1]), F32)
    for piece in range(PIECES):
        copies[1 + piece].wait()
        place = slice(piece * depth, (piece + 1) * depth)
        hidden += jnp.dot(feats_ref[:, place], first_ref[place], preferred_element_type=F32)
    hidden = jnp.maximum(hidden, 0.0).astype(BF16)
    copies[-1].wait()
    out = jnp.dot(hidden, second_ref[...], preferred_element_type=F32).astype(BF16)
    if unit:
        out = unit_of(out)
    for peer in range(out_ref.shape[0]):
        out_ref[peer] = out


def unit_kernel(mine_ref, other_ref, plain_ref, unit_ref):
    core = lax.axis_index("c")
    for half, got_ref in ((core, mine_ref), (1 - core, other_ref)):
        place = pl.ds(pl.multiple_of(half * HALF, HALF), HALF)
        plain = got_ref[...].reshape(HALF, LANES)
        plain_ref[place, :] = plain
        unit_ref[place, :] = unit_of(plain)


def row_totals(parts):
    return jnp.sum(parts.T, axis=0, keepdims=True)


def fill(out_ref, lines_ref):
    lines = lines_ref[...]
    for peer in range(PEERS):
        out_ref[peer] = lines


def tile_kernel(left_ref, right_ref, tile_ref, sums_ref, lines_ref):
    for step in range(PEERS // 2):
        left = left_ref[2 * step : 2 * step + 2].reshape(2 * LANES, LANES)
        rows = slice(step * 2 * LANES, (step + 1) * 2 * LANES)
        parts = jnp.zeros((2 * LANES, LANES), F32)
        for chunk in range(PEERS // 2):
            cols = slice(chunk * 2 * LANES, (chunk + 1) * 2 * LANES)
            dots = lax.dot_general(left, right_ref[cols], (((1,), (1,)), ((), ())), preferred_element_type=F32)
            block = jnp.exp2(dots * EXPONENT)
            tile_ref[rows, cols] = block
            parts += block[:, :LANES] + block[:, LANES:]
        lines_ref[2 * step : 2 * step + 1] = row_totals(parts[:LANES])
        lines_ref[2 * step + 1 : 2 * step + 2] = row_totals(parts[LANES:])
    fill(sums_ref, lines_ref)


def scale_of(got_ref):
    total = got_ref[0]
    for peer in range(1, PEERS):
        total += got_ref[peer]
    return 1.0 / total


def cols_kernel(got_ref, tile_ref, sums_ref, scale_ref, lines_ref):
    scale = scale_of(got_ref)
    scale_ref[...] = scale
    parts = [jnp.zeros((8, LANES), F32) for _ in range(PEERS)]
    for block in range(PEERS):
        rows = slice(block * LANES, (block + 1) * LANES)
        factor = jnp.broadcast_to(scale[block : block + 1], (LANES, LANES)).T
        for chunk in range(PEERS):
            product = tile_ref[rows, chunk * LANES : (chunk + 1) * LANES] * factor
            parts[chunk] += jnp.sum(product.reshape(LANES // 8, 8, LANES), axis=0)
    for chunk in range(PEERS):
        lines_ref[chunk : chunk + 1] = jnp.sum(parts[chunk], axis=0, keepdims=True)
    fill(sums_ref, lines_ref)


def rows_kernel(got_ref, tile_ref, sums_ref, lines_ref):
    scale = scale_of(got_ref)
    for block in range(PEERS):
        rows = slice(block * LANES, (block + 1) * LANES)
        parts = tile_ref[rows, :LANES] * scale[:1]
        for chunk in range(1, PEERS):
            parts += tile_ref[rows, chunk * LANES : (chunk + 1) * LANES] * scale[chunk : chunk + 1]
        lines_ref[block : block + 1] = row_totals(parts)
    fill(sums_ref, lines_ref)


def map_kernel(got_ref, tile_ref, plain_ref, out_ref):
    scale = scale_of(got_ref)
    wide = jnp.concatenate([scale[chunk : chunk + 1] for chunk in range(PEERS)], axis=1)
    scaled = (tile_ref[...] * wide).astype(BF16)
    part = jnp.dot(scaled, plain_ref[...], preferred_element_type=F32)
    out_ref[...] = part.reshape(PEERS, LANES, LANES).astype(BF16)


def finish_kernel(got_ref, scale_ref, out_ref):
    total = got_ref[0].astype(F32)
    for peer in range(1, PEERS):
        total += got_ref[peer].astype(F32)
    scale = scale_ref[pl.ds(lax.axis_index(SAME_ROWS), 1)]
    out_ref[...] = total * jnp.broadcast_to(scale, (LANES, LANES)).T


def call(kernel, outs, *args, scratch=(), flops=0, exps=0, limit=VMEM_LIMIT, **specs):
    moved = sum(math.prod(a.shape) * a.dtype.itemsize for a in args)
    return pl.pallas_call(
        kernel,
        out_shape=outs,
        **specs,
        scratch_shapes=scratch,
        compiler_params=pltpu.CompilerParams(vmem_limit_bytes=limit),
        cost_estimate=pl.CostEstimate(flops=flops, bytes_accessed=moved, transcendentals=exps),
    )(*args)


def near(array):
    return pltpu.with_memory_space_constraint(array, pltpu.VMEM)


def exchange(array, axes):
    return lax.all_to_all(array, axes, 0, 0)


def embed(feats, w_first, w_second, copies, unit):
    flops = 2 * feats.shape[0] * w_first.shape[0] * w_first.shape[1]
    return call(
        functools.partial(embed_kernel, unit=unit),
        pltpu.VMEM((copies, LANES, LANES), BF16),
        feats,
        w_first,
        w_second,
        in_specs=[pl.BlockSpec(memory_space=pltpu.HBM)] * 3,
        limit=60 * 2**20,
        scratch=(
            pltpu.VMEM(feats.shape, BF16),
            pltpu.VMEM(w_first.shape, BF16),
            pltpu.VMEM(w_second.shape, BF16),
            pltpu.SemaphoreType.DMA((PIECES + 2,)),
        ),
        flops=flops,
    )


def on_device(feats_one, feats_two, w_first, w_second):
    vectors = pltpu.VMEM((PEERS, PEERS, LANES), F32)
    lines = pltpu.VMEM((PEERS, LANES), F32)
    block = pltpu.VMEM((SIDE, LANES), BF16)
    plain_two = embed(feats_two, w_first, w_second, PEERS // 2, False)
    mine = exchange(plain_two, RING)
    unit_one = embed(feats_one, w_first, w_second, PEERS, True)
    mine, unit_one = lax.optimization_barrier((mine, unit_one))
    other = lax.ppermute(mine, "c", SWAP)
    units_left = exchange(unit_one, SAME_ROWS)
    plains, units_right = call(unit_kernel, (block, block), near(mine), near(other), flops=SIDE * LANES * 8)
    tile, sums = call(
        tile_kernel,
        (pltpu.VMEM((SIDE, SIDE), F32), vectors),
        near(units_left),
        near(units_right),
        scratch=(lines,),
        flops=2 * SIDE * SIDE * LANES,
        exps=SIDE * SIDE,
    )
    tile = near(tile)
    for sweep in range(SWEEPS):
        if sweep:
            sums = call(rows_kernel, vectors, sums, tile, scratch=(lines,))
        sums = near(exchange(sums, SAME_ROWS))
        sums, row_scale = call(cols_kernel, (vectors, lines), sums, tile, scratch=(lines,))
        sums = near(exchange(sums, SAME_COLS))
    parts = call(map_kernel, pltpu.VMEM((PEERS, LANES, LANES), BF16), sums, tile, near(plains))
    parts = near(exchange(parts, SAME_ROWS))
    return call(finish_kernel, jax.ShapeDtypeStruct((LANES, LANES), F32), parts, row_scale)


def solution(mesh):
    fine = Mesh(mesh.devices.reshape((2,) * 8), AXES)
    row, col = AXES[:4], AXES[4:]
    return jax.shard_map(
        on_device,
        mesh=fine,
        in_specs=(P(row + col, None), P(col + row, None), P(), P()),
        out_specs=P(row + col, None),
        check_vma=False,
    )
```

```python
import math

import jax
import jax.numpy as jnp
from jax import lax
from jax.experimental import pallas as pl
from jax.experimental.pallas import tpu as pltpu
from jax.sharding import Mesh
from jax.sharding import PartitionSpec as P

SWEEPS = 3
PIECES = 6
PEERS = 16
LANES = 128
SIDE = PEERS * LANES
EXPONENT = 20.0 * math.log2(math.e)
AXES = ("xh", "xl", "zh", "c", "yh", "yl", "zm", "zl")
SAME_ROWS = ("xh", "xl", "yh", "yl")
ALONG_X, ALONG_Y = SAME_ROWS[:2], SAME_ROWS[2:]
SIDES = 4
SAME_COLS = ("zh", "zm", "zl", "c")
RING = SAME_COLS[:3]
HALF = SIDE // 2
SWAP = [(0, 1), (1, 0)]
F32, BF16 = jnp.float32, jnp.bfloat16
VMEM_LIMIT = 16 * 2**20


def unit_of(plain):
    wide = plain.astype(F32)
    return (wide / jnp.sqrt(jnp.sum(wide * wide, axis=1, keepdims=True) + 1e-06)).astype(BF16)


def embed_kernel(one_hbm, two_hbm, first_hbm, second_hbm, unit_ref, plain_ref, feats_ref, first_ref, second_ref, sems):
    depth = first_hbm.shape[0] // PIECES
    copies = [
        pltpu.make_async_copy(one_hbm, feats_ref.at[pl.ds(0, LANES)], sems.at[PIECES]),
        pltpu.make_async_copy(two_hbm, feats_ref.at[pl.ds(LANES, LANES)], sems.at[PIECES + 1]),
    ]
    for piece in range(PIECES):
        place = pl.ds(piece * depth, depth)
        copies.append(pltpu.make_async_copy(first_hbm.at[place], first_ref.at[place], sems.at[piece]))
    copies.append(pltpu.make_async_copy(second_hbm, second_ref, sems.at[PIECES + 2]))
    for copy in copies:
        copy.start()
    copies[0].wait()
    copies[1].wait()
    hidden = None
    for piece in range(PIECES):
        copies[2 + piece].wait()
        place = slice(piece * depth, (piece + 1) * depth)
        part = jnp.dot(feats_ref[:, place], first_ref[place], preferred_element_type=F32)
        hidden = part if hidden is None else hidden + part
    hidden = jnp.maximum(hidden, 0.0).astype(BF16)
    copies[-1].wait()
    plain = jnp.dot(hidden, second_ref[...], preferred_element_type=F32).astype(BF16)
    unit_ref[...] = unit_of(plain[:LANES])
    for peer in range(plain_ref.shape[0]):
        plain_ref[peer] = plain[LANES:]


def unit_kernel(mine_ref, other_ref, plain_ref, unit_ref):
    core = lax.axis_index("c")
    for half, got_ref in ((core, mine_ref), (1 - core, other_ref)):
        place = pl.ds(pl.multiple_of(half * HALF, HALF), HALF)
        plain = got_ref[...].reshape(HALF, LANES)
        plain_ref[place, :] = plain
        unit_ref[place, :] = unit_of(plain)


def row_totals(parts):
    return jnp.sum(parts.T, axis=0, keepdims=True)


def fill(out_ref, lines_ref):
    lines = lines_ref[...].astype(out_ref.dtype)
    for peer in range(PEERS):
        out_ref[peer] = lines


def tile_kernel(*refs):
    *got_refs, right_ref, tile_ref, sums_ref, left_ref, lines_ref = refs
    for turn, got_ref in enumerate(got_refs):
        left_ref[turn * SIDES : (turn + 1) * SIDES] = got_ref[...]
    along_x, along_y = lax.axis_index(ALONG_X), lax.axis_index(ALONG_Y)

    def block_of(place):
        from_x, from_y = along_x ^ (place // SIDES), along_y ^ (place % SIDES)
        return left_ref[from_y * SIDES + from_x]

    for step in range(PEERS // 2):
        left = jnp.concatenate([block_of(2 * step), block_of(2 * step + 1)], axis=0)
        rows = slice(step * 2 * LANES, (step + 1) * 2 * LANES)
        parts = jnp.zeros((2 * LANES, LANES), F32)
        for chunk in range(PEERS // 2):
            cols = slice(chunk * 2 * LANES, (chunk + 1) * 2 * LANES)
            dots = lax.dot_general(left, right_ref[cols], (((1,), (1,)), ((), ())), preferred_element_type=F32)
            block = jnp.exp2(dots * EXPONENT)
            tile_ref[rows, cols] = block
            parts += block[:, :LANES] + block[:, LANES:]
        lines_ref[2 * step : 2 * step + 1] = row_totals(parts[:LANES])
        lines_ref[2 * step + 1 : 2 * step + 2] = row_totals(parts[LANES:])
    fill(sums_ref, lines_ref)


def scale_of(got_ref):
    total = got_ref[0].astype(F32)
    for peer in range(1, PEERS):
        total += got_ref[peer].astype(F32)
    return 1.0 / total


def cols_kernel(got_ref, tile_ref, sums_ref, scale_ref, lines_ref):
    scale = scale_of(got_ref)
    scale_ref[...] = scale
    parts = [jnp.zeros((8, LANES), F32) for _ in range(PEERS)]
    for block in range(PEERS):
        rows = slice(block * LANES, (block + 1) * LANES)
        factor = jnp.broadcast_to(scale[block : block + 1], (LANES, LANES)).T
        for chunk in range(PEERS):
            product = tile_ref[rows, chunk * LANES : (chunk + 1) * LANES] * factor
            parts[chunk] += jnp.sum(product.reshape(LANES // 8, 8, LANES), axis=0)
    for chunk in range(PEERS):
        lines_ref[chunk : chunk + 1] = jnp.sum(parts[chunk], axis=0, keepdims=True)
    fill(sums_ref, lines_ref)


def rows_kernel(got_ref, tile_ref, sums_ref, lines_ref):
    scale = scale_of(got_ref)
    for block in range(PEERS):
        rows = slice(block * LANES, (block + 1) * LANES)
        parts = tile_ref[rows, :LANES] * scale[:1]
        for chunk in range(1, PEERS):
            parts += tile_ref[rows, chunk * LANES : (chunk + 1) * LANES] * scale[chunk : chunk + 1]
        lines_ref[block : block + 1] = row_totals(parts)
    fill(sums_ref, lines_ref)


def map_kernel(got_ref, tile_ref, plain_ref, out_ref):
    scale = scale_of(got_ref)
    wide = jnp.concatenate([scale[chunk : chunk + 1] for chunk in range(PEERS)], axis=1)
    scaled = (tile_ref[...] * wide).astype(BF16)
    part = jnp.dot(scaled, plain_ref[...], preferred_element_type=F32)
    out_ref[...] = part.reshape(PEERS, LANES, LANES).astype(BF16)


def finish_kernel(got_ref, scale_ref, out_ref):
    total = got_ref[0].astype(F32)
    for peer in range(1, PEERS):
        total += got_ref[peer].astype(F32)
    scale = scale_ref[pl.ds(lax.axis_index(SAME_ROWS), 1)]
    out_ref[...] = total * jnp.broadcast_to(scale, (LANES, LANES)).T


def call(kernel, outs, *args, scratch=(), flops=0, exps=0, limit=VMEM_LIMIT, **specs):
    moved = sum(math.prod(a.shape) * a.dtype.itemsize for a in args)
    return pl.pallas_call(
        kernel,
        out_shape=outs,
        **specs,
        scratch_shapes=scratch,
        compiler_params=pltpu.CompilerParams(vmem_limit_bytes=limit),
        cost_estimate=pl.CostEstimate(flops=flops, bytes_accessed=moved, transcendentals=exps),
    )(*args)


def near(array):
    return pltpu.with_memory_space_constraint(array, pltpu.VMEM)


def exchange(array, axes):
    return lax.all_to_all(array, axes, 0, 0)


def turned(array, axes):
    swaps = [[(place, place ^ turn) for place in range(SIDES)] for turn in range(1, SIDES)]
    return [array] + [lax.ppermute(array, axes, swap) for swap in swaps]


def on_device(feats_one, feats_two, w_first, w_second):
    short = pltpu.VMEM((PEERS, PEERS, LANES), BF16)
    wide = pltpu.VMEM((PEERS, PEERS, LANES), F32)
    lines = pltpu.VMEM((PEERS, LANES), F32)
    block = pltpu.VMEM((SIDE, LANES), BF16)
    unit_one, plain_two = call(
        embed_kernel,
        (pltpu.VMEM((LANES, LANES), BF16), pltpu.VMEM((PEERS // 2, LANES, LANES), BF16)),
        feats_one,
        feats_two,
        w_first,
        w_second,
        in_specs=[pl.BlockSpec(memory_space=pltpu.HBM)] * 4,
        limit=60 * 2**20,
        scratch=(
            pltpu.VMEM((2 * LANES, feats_one.shape[1]), BF16),
            pltpu.VMEM(w_first.shape, BF16),
            pltpu.VMEM(w_second.shape, BF16),
            pltpu.SemaphoreType.DMA((PIECES + 3,)),
        ),
        flops=4 * LANES * w_first.shape[0] * w_first.shape[1],
    )
    mine = exchange(plain_two, RING)
    other = lax.ppermute(mine, "c", SWAP)
    strip = jnp.stack(turned(unit_one, ALONG_X))
    units_left = [near(part) for part in turned(strip, ALONG_Y)]
    plains, units_right = call(unit_kernel, (block, block), near(mine), near(other), flops=SIDE * LANES * 8)
    tile, sums = call(
        tile_kernel,
        (pltpu.VMEM((SIDE, SIDE), F32), short),
        *units_left,
        near(units_right),
        scratch=(pltpu.VMEM((PEERS, LANES, LANES), BF16), lines),
        flops=2 * SIDE * SIDE * LANES,
        exps=SIDE * SIDE,
    )
    tile = near(tile)
    for sweep in range(SWEEPS):
        if sweep:
            sums = call(rows_kernel, short, sums, tile, scratch=(lines,))
        sums = near(exchange(sums, SAME_ROWS))
        totals = wide if sweep == SWEEPS - 1 else short
        sums, row_scale = call(cols_kernel, (totals, lines), sums, tile, scratch=(lines,))
        sums = near(exchange(sums, SAME_COLS))
    parts = call(map_kernel, pltpu.VMEM((PEERS, LANES, LANES), BF16), sums, tile, near(plains))
    parts = near(exchange(parts, SAME_ROWS))
    return call(finish_kernel, jax.ShapeDtypeStruct((LANES, LANES), F32), parts, row_scale)


def solution(mesh):
    fine = Mesh(mesh.devices.reshape((2,) * 8), AXES)
    row, col = AXES[:4], AXES[4:]
    return jax.shard_map(
        on_device,
        mesh=fine,
        in_specs=(P(row + col, None), P(col + row, None), P(), P()),
        out_specs=P(row + col, None),
        check_vma=False,
    )
```

```python
import math

import jax
import jax.numpy as jnp
from jax import lax
from jax.experimental import pallas as pl
from jax.experimental.pallas import tpu as pltpu
from jax.sharding import Mesh
from jax.sharding import PartitionSpec as P

SWEEPS = 3
PIECES = 6
PEERS = 16
LANES = 128
SIDE = PEERS * LANES
EXPONENT = 20.0 * math.log2(math.e)
AXES = ("xh", "xl", "zh", "c", "yh", "yl", "zm", "zl")
SAME_ROWS = ("xh", "xl", "yh", "yl")
ALONG_X, ALONG_Y = SAME_ROWS[:2], SAME_ROWS[2:]
SIDES = 4
SAME_COLS = ("zh", "zm", "zl", "c")
RING = SAME_COLS[:3]
HALF = SIDE // 2
SWAP = [(0, 1), (1, 0)]
F32, BF16 = jnp.float32, jnp.bfloat16
VMEM_LIMIT = 16 * 2**20


def unit_of(plain):
    wide = plain.astype(F32)
    return (wide / jnp.sqrt(jnp.sum(wide * wide, axis=1, keepdims=True) + 1e-06)).astype(BF16)


def embed_kernel(one_hbm, two_hbm, first_hbm, second_hbm, unit_ref, plain_ref, feats_ref, first_ref, second_ref, sems):
    depth = first_hbm.shape[0] // PIECES
    copies = [
        pltpu.make_async_copy(one_hbm, feats_ref.at[pl.ds(0, LANES)], sems.at[PIECES]),
        pltpu.make_async_copy(two_hbm, feats_ref.at[pl.ds(LANES, LANES)], sems.at[PIECES + 1]),
    ]
    for piece in range(PIECES):
        place = pl.ds(piece * depth, depth)
        copies.append(pltpu.make_async_copy(first_hbm.at[place], first_ref.at[place], sems.at[piece]))
    copies.append(pltpu.make_async_copy(second_hbm, second_ref, sems.at[PIECES + 2]))
    for copy in copies:
        copy.start()
    copies[0].wait()
    copies[1].wait()
    hidden = None
    for piece in range(PIECES):
        copies[2 + piece].wait()
        place = slice(piece * depth, (piece + 1) * depth)
        part = jnp.dot(feats_ref[:, place], first_ref[place], preferred_element_type=F32)
        hidden = part if hidden is None else hidden + part
    hidden = jnp.maximum(hidden, 0.0).astype(BF16)
    copies[-1].wait()
    plain = jnp.dot(hidden, second_ref[...], preferred_element_type=F32).astype(BF16)
    unit_ref[...] = unit_of(plain[:LANES])
    for peer in range(plain_ref.shape[0]):
        plain_ref[peer] = plain[LANES:]


def row_totals(parts):
    return jnp.sum(parts.T, axis=0, keepdims=True)


def fill(out_ref, lines_ref):
    lines = lines_ref[...].astype(out_ref.dtype)
    for peer in range(PEERS):
        out_ref[peer] = lines


def half_tile(left_ref, plain_ref, tile_ref, units_ref, lines_ref):
    units_ref[...] = unit_of(plain_ref[...].reshape(HALF, LANES))
    for step in range(PEERS // 2):
        left = left_ref[2 * step : 2 * step + 2].reshape(2 * LANES, LANES)
        rows = slice(step * 2 * LANES, (step + 1) * 2 * LANES)
        parts = jnp.zeros((2 * LANES, LANES), F32)
        for chunk in range(PEERS // 4):
            cols = slice(chunk * 2 * LANES, (chunk + 1) * 2 * LANES)
            dots = lax.dot_general(left, units_ref[cols], (((1,), (1,)), ((), ())), preferred_element_type=F32)
            block = jnp.exp2(dots * EXPONENT)
            tile_ref[rows, cols] = block
            parts += block[:, :LANES] + block[:, LANES:]
        lines_ref[2 * step : 2 * step + 1] = row_totals(parts[:LANES])
        lines_ref[2 * step + 1 : 2 * step + 2] = row_totals(parts[LANES:])


def mine_kernel(*refs):
    *got_refs, plain_ref, tile_ref, left_ref, lines_ref, held_ref, units_ref = refs
    for turn, got_ref in enumerate(got_refs):
        held_ref[turn * SIDES : (turn + 1) * SIDES] = got_ref[...]
    along_x, along_y = lax.axis_index(ALONG_X), lax.axis_index(ALONG_Y)
    for place in range(PEERS):
        from_x, from_y = along_x ^ (place // SIDES), along_y ^ (place % SIDES)
        left_ref[place] = held_ref[from_y * SIDES + from_x]
    half_tile(left_ref, plain_ref, tile_ref, units_ref, lines_ref)


def other_kernel(left_ref, plain_ref, first_ref, tile_ref, sums_ref, units_ref, lines_ref):
    half_tile(left_ref, plain_ref, tile_ref, units_ref, lines_ref)
    lines_ref[...] += first_ref[...]
    fill(sums_ref, lines_ref)


def core_lines():
    core = lax.axis_index("c")
    return [pl.ds(pl.multiple_of(half * (PEERS // 2), PEERS // 2), PEERS // 2) for half in (core, 1 - core)]


def scale_of(got_ref):
    total = got_ref[0].astype(F32)
    for peer in range(1, PEERS):
        total += got_ref[peer].astype(F32)
    return 1.0 / total


def cols_kernel(got_ref, mine_ref, other_ref, sums_ref, scale_ref, lines_ref):
    scale = scale_of(got_ref)
    scale_ref[...] = scale
    chunks = PEERS // 2
    parts = [jnp.zeros((8, LANES), F32) for _ in range(PEERS)]
    for block in range(PEERS):
        rows = slice(block * LANES, (block + 1) * LANES)
        factor = jnp.broadcast_to(scale[block : block + 1], (LANES, LANES)).T
        for chunk in range(PEERS):
            half_ref, at = (mine_ref, other_ref)[chunk // chunks], chunk % chunks
            product = half_ref[rows, at * LANES : (at + 1) * LANES] * factor
            parts[chunk] += jnp.sum(product.reshape(LANES // 8, 8, LANES), axis=0)
    lines = [jnp.sum(part, axis=0, keepdims=True) for part in parts]
    for half, place in enumerate(core_lines()):
        lines_ref[place] = jnp.concatenate(lines[half * chunks : (half + 1) * chunks], axis=0)
    fill(sums_ref, lines_ref)


def local_scale(got_ref, lines_ref):
    lines_ref[...] = scale_of(got_ref)
    halves = [lines_ref[place] for place in core_lines()]
    return [half[row : row + 1] for half in halves for row in range(PEERS // 2)]


def rows_kernel(got_ref, mine_ref, other_ref, sums_ref, lines_ref):
    scale = local_scale(got_ref, lines_ref)
    for block in range(PEERS):
        rows = slice(block * LANES, (block + 1) * LANES)
        parts = None
        for chunk in range(PEERS):
            half_ref, at = (mine_ref, other_ref)[2 * chunk // PEERS], chunk % (PEERS // 2)
            product = half_ref[rows, at * LANES : (at + 1) * LANES] * scale[chunk]
            parts = product if parts is None else parts + product
        lines_ref[block : block + 1] = row_totals(parts)
    fill(sums_ref, lines_ref)


def map_kernel(got_ref, mine_ref, other_ref, plain_mine_ref, plain_other_ref, out_ref, lines_ref):
    scale = local_scale(got_ref, lines_ref)
    part = None
    for half, (tile_ref, plain_ref) in enumerate(((mine_ref, plain_mine_ref), (other_ref, plain_other_ref))):
        wide = jnp.concatenate(scale[half * PEERS // 2 : (half + 1) * PEERS // 2], axis=1)
        scaled = (tile_ref[...] * wide).astype(BF16)
        plain = plain_ref[...].reshape(HALF, LANES)
        product = jnp.dot(scaled, plain, preferred_element_type=F32)
        part = product if part is None else part + product
    out_ref[...] = part.reshape(PEERS, LANES, LANES).astype(BF16)


def finish_kernel(got_ref, scale_ref, out_ref):
    total = got_ref[0].astype(F32)
    for peer in range(1, PEERS):
        total += got_ref[peer].astype(F32)
    scale = scale_ref[pl.ds(lax.axis_index(SAME_ROWS), 1)]
    out_ref[...] = total * jnp.broadcast_to(scale, (LANES, LANES)).T


def call(kernel, outs, *args, scratch=(), flops=0, exps=0, limit=VMEM_LIMIT, **specs):
    moved = sum(math.prod(a.shape) * a.dtype.itemsize for a in args)
    return pl.pallas_call(
        kernel,
        out_shape=outs,
        **specs,
        scratch_shapes=scratch,
        compiler_params=pltpu.CompilerParams(vmem_limit_bytes=limit),
        cost_estimate=pl.CostEstimate(flops=flops, bytes_accessed=moved, transcendentals=exps),
    )(*args)


def near(array):
    return pltpu.with_memory_space_constraint(array, pltpu.VMEM)


def exchange(array, axes):
    return lax.all_to_all(array, axes, 0, 0)


def turned(array, axes):
    swaps = [[(place, place ^ turn) for place in range(SIDES)] for turn in range(1, SIDES)]
    return [array] + [lax.ppermute(array, axes, swap) for swap in swaps]


def on_device(feats_one, feats_two, w_first, w_second):
    short = pltpu.VMEM((PEERS, PEERS, LANES), BF16)
    wide = pltpu.VMEM((PEERS, PEERS, LANES), F32)
    lines = pltpu.VMEM((PEERS, LANES), F32)
    unit_one, plain_two = call(
        embed_kernel,
        (pltpu.VMEM((LANES, LANES), BF16), pltpu.VMEM((PEERS // 2, LANES, LANES), BF16)),
        feats_one,
        feats_two,
        w_first,
        w_second,
        in_specs=[pl.BlockSpec(memory_space=pltpu.HBM)] * 4,
        limit=60 * 2**20,
        scratch=(
            pltpu.VMEM((2 * LANES, feats_one.shape[1]), BF16),
            pltpu.VMEM(w_first.shape, BF16),
            pltpu.VMEM(w_second.shape, BF16),
            pltpu.SemaphoreType.DMA((PIECES + 3,)),
        ),
        flops=4 * LANES * w_first.shape[0] * w_first.shape[1],
    )
    mine = exchange(plain_two, RING)
    strip = jnp.stack(turned(unit_one, ALONG_X))
    mine, *units_left = lax.optimization_barrier((mine, *turned(strip, ALONG_Y)))
    units_left = [near(part) for part in units_left]
    other = lax.ppermute(mine, "c", SWAP)
    half, units = pltpu.VMEM((SIDE, HALF), F32), pltpu.VMEM((HALF, LANES), BF16)
    blocks = pltpu.VMEM((PEERS, LANES, LANES), BF16)
    work = dict(flops=2 * SIDE * HALF * LANES, exps=SIDE * HALF)
    mine, other = near(mine), near(other)
    tile_mine, left, first = call(mine_kernel, (half, blocks, lines), *units_left, mine, scratch=(blocks, units), **work)
    tile_other, sums = call(other_kernel, (half, short), near(left), other, near(first), scratch=(units, lines), **work)
    tile = (near(tile_mine), near(tile_other))
    for sweep in range(SWEEPS):
        if sweep:
            sums = call(rows_kernel, short, sums, *tile, scratch=(lines,))
        sums = near(exchange(sums, SAME_ROWS))
        totals = wide if sweep == SWEEPS - 1 else short
        sums, row_scale = call(cols_kernel, (totals, lines), sums, *tile, scratch=(lines,))
        sums = near(exchange(sums, SAME_COLS))
    parts = call(map_kernel, blocks, sums, *tile, mine, other, scratch=(lines,))
    parts = near(exchange(parts, SAME_ROWS))
    return call(finish_kernel, jax.ShapeDtypeStruct((LANES, LANES), F32), parts, row_scale)


def solution(mesh):
    fine = Mesh(mesh.devices.reshape((2,) * 8), AXES)
    row, col = AXES[:4], AXES[4:]
    return jax.shard_map(
        on_device,
        mesh=fine,
        in_specs=(P(row + col, None), P(col + row, None), P(), P()),
        out_specs=P(row + col, None),
        check_vma=False,
    )
```

```python
import math

import jax
import jax.numpy as jnp
from jax import lax
from jax.experimental import pallas as pl
from jax.experimental.pallas import tpu as pltpu
from jax.sharding import Mesh
from jax.sharding import PartitionSpec as P

SWEEPS = 3
PIECES = 6
FLOPS_HINT = 10**9
PEERS = 16
LANES = 128
SIDE = PEERS * LANES
EXPONENT = 20.0 * math.log2(math.e)
AXES = ("xh", "xl", "zh", "c", "yh", "yl", "zm", "zl")
SAME_ROWS = ("xh", "xl", "yh", "yl")
ALONG_X, ALONG_Y = SAME_ROWS[:2], SAME_ROWS[2:]
SIDES = 4
SAME_COLS = ("zh", "zm", "zl", "c")
RING = SAME_COLS[:3]
HALF = SIDE // 2
SWAP = [(0, 1), (1, 0)]
F32, BF16 = jnp.float32, jnp.bfloat16
VMEM_LIMIT = 16 * 2**20


def unit_of(plain):
    wide = plain.astype(F32)
    return (wide / jnp.sqrt(jnp.sum(wide * wide, axis=1, keepdims=True) + 1e-06)).astype(BF16)


def embed_kernel(one_hbm, two_hbm, first_hbm, second_hbm, unit_ref, plain_ref, feats_ref, first_ref, second_ref, sems):
    depth = first_hbm.shape[0] // PIECES
    copies = [
        pltpu.make_async_copy(one_hbm, feats_ref.at[pl.ds(0, LANES)], sems.at[PIECES]),
        pltpu.make_async_copy(two_hbm, feats_ref.at[pl.ds(LANES, LANES)], sems.at[PIECES + 1]),
    ]
    for piece in range(PIECES):
        place = pl.ds(piece * depth, depth)
        copies.append(pltpu.make_async_copy(first_hbm.at[place], first_ref.at[place], sems.at[piece]))
    copies.append(pltpu.make_async_copy(second_hbm, second_ref, sems.at[PIECES + 2]))
    for copy in copies:
        copy.start()
    copies[0].wait()
    copies[1].wait()
    hidden = None
    for piece in range(PIECES):
        copies[2 + piece].wait()
        place = slice(piece * depth, (piece + 1) * depth)
        part = jnp.dot(feats_ref[:, place], first_ref[place], preferred_element_type=F32)
        hidden = part if hidden is None else hidden + part
    hidden = jnp.maximum(hidden, 0.0).astype(BF16)
    copies[-1].wait()
    plain = jnp.dot(hidden, second_ref[...], preferred_element_type=F32).astype(BF16)
    unit_ref[...] = unit_of(plain[:LANES])
    for peer in range(plain_ref.shape[0]):
        plain_ref[peer] = plain[LANES:]


def row_totals(parts):
    return jnp.sum(parts.T, axis=0, keepdims=True)


def fill(out_ref, lines_ref):
    lines = lines_ref[...].astype(out_ref.dtype)
    for peer in range(PEERS):
        out_ref[peer] = lines


def half_tile(left_ref, rows_ref, tile_ref, lines_ref):
    for step in range(PEERS // 2):
        left = left_ref[2 * step : 2 * step + 2].reshape(2 * LANES, LANES)
        rows = slice(step * 2 * LANES, (step + 1) * 2 * LANES)
        parts = jnp.zeros((2 * LANES, LANES), F32)
        for chunk in range(PEERS // 4):
            cols = slice(chunk * 2 * LANES, (chunk + 1) * 2 * LANES)
            dots = lax.dot_general(left, rows_ref[0, cols], (((1,), (1,)), ((), ())), preferred_element_type=F32)
            block = jnp.exp2(dots * EXPONENT)
            tile_ref[rows, cols] = block
            parts += block[:, :LANES] + block[:, LANES:]
        lines_ref[2 * step : 2 * step + 1] = row_totals(parts[:LANES])
        lines_ref[2 * step + 1 : 2 * step + 2] = row_totals(parts[LANES:])


def unit_kernel(plain_ref, rows_ref):
    plain = plain_ref[...].reshape(HALF, LANES)
    rows_ref[0] = unit_of(plain)
    rows_ref[1] = plain


def mine_kernel(*refs):
    *got_refs, rows_ref, tile_ref, left_ref, lines_ref, held_ref = refs
    for turn, got_ref in enumerate(got_refs):
        held_ref[turn * SIDES : (turn + 1) * SIDES] = got_ref[...]
    along_x, along_y = lax.axis_index(ALONG_X), lax.axis_index(ALONG_Y)
    for place in range(PEERS):
        from_x, from_y = along_x ^ (place // SIDES), along_y ^ (place % SIDES)
        left_ref[place] = held_ref[from_y * SIDES + from_x]
    half_tile(left_ref, rows_ref, tile_ref, lines_ref)


def other_kernel(left_ref, rows_ref, first_ref, tile_ref, sums_ref, lines_ref):
    half_tile(left_ref, rows_ref, tile_ref, lines_ref)
    lines_ref[...] += first_ref[...]
    fill(sums_ref, lines_ref)


def core_lines():
    core = lax.axis_index("c")
    return [pl.ds(pl.multiple_of(half * (PEERS // 2), PEERS // 2), PEERS // 2) for half in (core, 1 - core)]


def scale_of(got_ref):
    total = got_ref[0].astype(F32)
    for peer in range(1, PEERS):
        total += got_ref[peer].astype(F32)
    return 1.0 / total


def cols_kernel(got_ref, mine_ref, other_ref, sums_ref, scale_ref, lines_ref):
    scale = scale_of(got_ref)
    scale_ref[...] = scale
    chunks = PEERS // 2
    parts = [jnp.zeros((8, LANES), F32) for _ in range(PEERS)]
    for block in range(PEERS):
        rows = slice(block * LANES, (block + 1) * LANES)
        factor = jnp.broadcast_to(scale[block : block + 1], (LANES, LANES)).T
        for chunk in range(PEERS):
            half_ref, at = (mine_ref, other_ref)[chunk // chunks], chunk % chunks
            product = half_ref[rows, at * LANES : (at + 1) * LANES] * factor
            parts[chunk] += jnp.sum(product.reshape(LANES // 8, 8, LANES), axis=0)
    lines = [jnp.sum(part, axis=0, keepdims=True) for part in parts]
    for half, place in enumerate(core_lines()):
        lines_ref[place] = jnp.concatenate(lines[half * chunks : (half + 1) * chunks], axis=0)
    fill(sums_ref, lines_ref)


def local_scale(got_ref, lines_ref):
    lines_ref[...] = scale_of(got_ref)
    halves = [lines_ref[place] for place in core_lines()]
    return [half[row : row + 1] for half in halves for row in range(PEERS // 2)]


def rows_kernel(got_ref, mine_ref, other_ref, sums_ref, lines_ref):
    scale = local_scale(got_ref, lines_ref)
    for block in range(PEERS):
        rows = slice(block * LANES, (block + 1) * LANES)
        parts = None
        for chunk in range(PEERS):
            half_ref, at = (mine_ref, other_ref)[2 * chunk // PEERS], chunk % (PEERS // 2)
            product = half_ref[rows, at * LANES : (at + 1) * LANES] * scale[chunk]
            parts = product if parts is None else parts + product
        lines_ref[block : block + 1] = row_totals(parts)
    fill(sums_ref, lines_ref)


def map_kernel(got_ref, mine_ref, other_ref, plain_mine_ref, plain_other_ref, out_ref, lines_ref):
    scale = local_scale(got_ref, lines_ref)
    part = None
    for half, (tile_ref, plain_ref) in enumerate(((mine_ref, plain_mine_ref), (other_ref, plain_other_ref))):
        wide = jnp.concatenate(scale[half * PEERS // 2 : (half + 1) * PEERS // 2], axis=1)
        scaled = (tile_ref[...] * wide).astype(BF16)
        product = jnp.dot(scaled, plain_ref[1], preferred_element_type=F32)
        part = product if part is None else part + product
    out_ref[...] = part.reshape(PEERS, LANES, LANES).astype(BF16)


def finish_kernel(got_ref, scale_ref, out_ref):
    total = got_ref[0].astype(F32)
    for peer in range(1, PEERS):
        total += got_ref[peer].astype(F32)
    scale = scale_ref[pl.ds(lax.axis_index(SAME_ROWS), 1)]
    out_ref[...] = total * jnp.broadcast_to(scale, (LANES, LANES)).T


def call(kernel, outs, *args, scratch=(), flops=0, exps=0, limit=VMEM_LIMIT, **specs):
    moved = sum(math.prod(a.shape) * a.dtype.itemsize for a in args)
    return pl.pallas_call(
        kernel,
        out_shape=outs,
        **specs,
        scratch_shapes=scratch,
        compiler_params=pltpu.CompilerParams(vmem_limit_bytes=limit),
        cost_estimate=pl.CostEstimate(flops=flops, bytes_accessed=moved, transcendentals=exps),
    )(*args)


def near(array):
    return pltpu.with_memory_space_constraint(array, pltpu.VMEM)


def exchange(array, axes):
    return lax.all_to_all(array, axes, 0, 0)


def turned(array, axes):
    swaps = [[(place, place ^ turn) for place in range(SIDES)] for turn in range(1, SIDES)]
    return [array] + [lax.ppermute(array, axes, swap) for swap in swaps]


def on_device(feats_one, feats_two, w_first, w_second):
    short = pltpu.VMEM((PEERS, PEERS, LANES), BF16)
    wide = pltpu.VMEM((PEERS, PEERS, LANES), F32)
    lines = pltpu.VMEM((PEERS, LANES), F32)
    unit_one, plain_two = call(
        embed_kernel,
        (pltpu.VMEM((LANES, LANES), BF16), pltpu.VMEM((PEERS // 2, LANES, LANES), BF16)),
        feats_one,
        feats_two,
        w_first,
        w_second,
        in_specs=[pl.BlockSpec(memory_space=pltpu.HBM)] * 4,
        limit=60 * 2**20,
        scratch=(
            pltpu.VMEM((2 * LANES, feats_one.shape[1]), BF16),
            pltpu.VMEM(w_first.shape, BF16),
            pltpu.VMEM(w_second.shape, BF16),
            pltpu.SemaphoreType.DMA((PIECES + 3,)),
        ),
        flops=4 * LANES * w_first.shape[0] * w_first.shape[1],
    )
    mine = exchange(plain_two, RING)
    strip = jnp.stack(turned(unit_one, ALONG_X))
    half = pltpu.VMEM((SIDE, HALF), F32)
    blocks = pltpu.VMEM((PEERS, LANES, LANES), BF16)
    work = dict(flops=2 * SIDE * HALF * LANES, exps=SIDE * HALF)
    mine = call(unit_kernel, pltpu.VMEM((2, HALF, LANES), BF16), near(mine), flops=FLOPS_HINT)
    mine, *units_left = lax.optimization_barrier((mine, *turned(strip, ALONG_Y)))
    units_left = [near(part) for part in units_left]
    other = near(lax.ppermute(mine, "c", SWAP))
    mine = near(mine)
    tile_mine, left, first = call(mine_kernel, (half, blocks, lines), *units_left, mine, scratch=(blocks,), **work)
    tile_other, sums = call(other_kernel, (half, short), near(left), other, near(first), scratch=(lines,), **work)
    tile = (near(tile_mine), near(tile_other))
    for sweep in range(SWEEPS):
        if sweep:
            sums = call(rows_kernel, short, sums, *tile, scratch=(lines,))
        sums = near(exchange(sums, SAME_ROWS))
        totals = wide if sweep == SWEEPS - 1 else short
        sums, row_scale = call(cols_kernel, (totals, lines), sums, *tile, scratch=(lines,))
        sums = near(exchange(sums, SAME_COLS))
    parts = call(map_kernel, blocks, sums, *tile, mine, other, scratch=(lines,))
    parts = near(exchange(parts, SAME_ROWS))
    return call(finish_kernel, jax.ShapeDtypeStruct((LANES, LANES), F32), parts, row_scale)


def solution(mesh):
    fine = Mesh(mesh.devices.reshape((2,) * 8), AXES)
    row, col = AXES[:4], AXES[4:]
    return jax.shard_map(
        on_device,
        mesh=fine,
        in_specs=(P(row + col, None), P(col + row, None), P(), P()),
        out_specs=P(row + col, None),
        check_vma=False,
    )
```

```python
import math

import jax
import jax.numpy as jnp
from jax import lax
from jax.experimental import pallas as pl
from jax.experimental.pallas import tpu as pltpu
from jax.sharding import Mesh
from jax.sharding import PartitionSpec as P

SWEEPS = 3
PIECES = 6
FLOPS_HINT = 10**9
PEERS = 16
LANES = 128
SIDE = PEERS * LANES
EXPONENT = 20.0 * math.log2(math.e)
AXES = ("xh", "xl", "zh", "c", "yh", "yl", "zm", "zl")
SAME_ROWS = ("xh", "xl", "yh", "yl")
ALONG_X, ALONG_Y = SAME_ROWS[:2], SAME_ROWS[2:]
SIDES = 4
SAME_COLS = ("c", "zh", "zm", "zl")
RING = SAME_COLS[1:]
HALF = SIDE // 2
SWAP = [(0, 1), (1, 0)]
F32, BF16 = jnp.float32, jnp.bfloat16
VMEM_LIMIT = 16 * 2**20


def unit_of(plain):
    wide = plain.astype(F32)
    return (wide / jnp.sqrt(jnp.sum(wide * wide, axis=1, keepdims=True) + 1e-06)).astype(BF16)


def embed_kernel(one_hbm, two_hbm, first_hbm, second_hbm, unit_ref, plain_ref, feats_ref, first_ref, second_ref, sems):
    depth = first_hbm.shape[0] // PIECES
    copies = [
        pltpu.make_async_copy(one_hbm, feats_ref.at[pl.ds(0, LANES)], sems.at[PIECES]),
        pltpu.make_async_copy(two_hbm, feats_ref.at[pl.ds(LANES, LANES)], sems.at[PIECES + 1]),
    ]
    for piece in range(PIECES):
        place = pl.ds(piece * depth, depth)
        copies.append(pltpu.make_async_copy(first_hbm.at[place], first_ref.at[place], sems.at[piece]))
    copies.append(pltpu.make_async_copy(second_hbm, second_ref, sems.at[PIECES + 2]))
    for copy in copies:
        copy.start()
    copies[0].wait()
    copies[1].wait()
    hidden = None
    for piece in range(PIECES):
        copies[2 + piece].wait()
        place = slice(piece * depth, (piece + 1) * depth)
        part = jnp.dot(feats_ref[:, place], first_ref[place], preferred_element_type=F32)
        hidden = part if hidden is None else hidden + part
    hidden = jnp.maximum(hidden, 0.0).astype(BF16)
    copies[-1].wait()
    plain = jnp.dot(hidden, second_ref[...], preferred_element_type=F32).astype(BF16)
    unit_ref[...] = unit_of(plain[:LANES])
    for peer in range(plain_ref.shape[0]):
        plain_ref[peer] = plain[LANES:]


def row_totals(parts):
    return jnp.sum(parts.T, axis=0, keepdims=True)


def fill(out_ref, lines_ref):
    lines = lines_ref[...].astype(out_ref.dtype)
    for peer in range(PEERS):
        out_ref[peer] = lines


def half_tile(left_ref, rows_ref, tile_ref, lines_ref):
    for step in range(PEERS // 2):
        left = left_ref[2 * step : 2 * step + 2].reshape(2 * LANES, LANES)
        rows = slice(step * 2 * LANES, (step + 1) * 2 * LANES)
        parts = jnp.zeros((2 * LANES, LANES), F32)
        for chunk in range(PEERS // 4):
            cols = slice(chunk * 2 * LANES, (chunk + 1) * 2 * LANES)
            dots = lax.dot_general(left, rows_ref[0, cols], (((1,), (1,)), ((), ())), preferred_element_type=F32)
            block = jnp.exp2(dots * EXPONENT)
            tile_ref[rows, cols] = block
            parts += block[:, :LANES] + block[:, LANES:]
        lines_ref[2 * step : 2 * step + 1] = row_totals(parts[:LANES])
        lines_ref[2 * step + 1 : 2 * step + 2] = row_totals(parts[LANES:])


def unit_kernel(plain_ref, rows_ref):
    plain = plain_ref[...].reshape(HALF, LANES)
    rows_ref[0] = unit_of(plain)
    rows_ref[1] = plain


def mine_kernel(*refs):
    *got_refs, rows_ref, tile_ref, left_ref, lines_ref, held_ref = refs
    for turn, got_ref in enumerate(got_refs):
        held_ref[turn * SIDES : (turn + 1) * SIDES] = got_ref[...]
    along_x, along_y = lax.axis_index(ALONG_X), lax.axis_index(ALONG_Y)
    for place in range(PEERS):
        from_x, from_y = along_x ^ (place // SIDES), along_y ^ (place % SIDES)
        left_ref[place] = held_ref[from_y * SIDES + from_x]
    half_tile(left_ref, rows_ref, tile_ref, lines_ref)


def other_kernel(left_ref, rows_ref, first_ref, tile_ref, sums_ref, lines_ref):
    half_tile(left_ref, rows_ref, tile_ref, lines_ref)
    lines_ref[...] += first_ref[...]
    fill(sums_ref, lines_ref)


def core_lines():
    core = lax.axis_index("c")
    return [pl.ds(pl.multiple_of(half * (PEERS // 2), PEERS // 2), PEERS // 2) for half in (core, 1 - core)]


def scale_of(got_ref):
    total = got_ref[0].astype(F32)
    for peer in range(1, PEERS):
        total += got_ref[peer].astype(F32)
    return 1.0 / total


def cols_kernel(got_ref, mine_ref, other_ref, sums_ref, scale_ref, lines_ref):
    scale = scale_of(got_ref)
    scale_ref[...] = scale
    chunks = PEERS // 2
    parts = [jnp.zeros((8, LANES), F32) for _ in range(PEERS)]
    for block in range(PEERS):
        rows = slice(block * LANES, (block + 1) * LANES)
        factor = jnp.broadcast_to(scale[block : block + 1], (LANES, LANES)).T
        for chunk in range(PEERS):
            half_ref, at = (mine_ref, other_ref)[chunk // chunks], chunk % chunks
            product = half_ref[rows, at * LANES : (at + 1) * LANES] * factor
            parts[chunk] += jnp.sum(product.reshape(LANES // 8, 8, LANES), axis=0)
    lines = [jnp.sum(part, axis=0, keepdims=True) for part in parts]
    for half, place in enumerate(core_lines()):
        lines_ref[place] = jnp.concatenate(lines[half * chunks : (half + 1) * chunks], axis=0)
    fill(sums_ref, lines_ref)


def local_scale(got_ref, lines_ref):
    lines_ref[...] = scale_of(got_ref)
    halves = [lines_ref[place] for place in core_lines()]
    return [half[row : row + 1] for half in halves for row in range(PEERS // 2)]


def rows_kernel(got_ref, mine_ref, other_ref, sums_ref, lines_ref):
    scale = local_scale(got_ref, lines_ref)
    for block in range(PEERS):
        rows = slice(block * LANES, (block + 1) * LANES)
        parts = None
        for chunk in range(PEERS):
            half_ref, at = (mine_ref, other_ref)[2 * chunk // PEERS], chunk % (PEERS // 2)
            product = half_ref[rows, at * LANES : (at + 1) * LANES] * scale[chunk]
            parts = product if parts is None else parts + product
        lines_ref[block : block + 1] = row_totals(parts)
    fill(sums_ref, lines_ref)


def map_kernel(got_ref, mine_ref, other_ref, plain_mine_ref, plain_other_ref, out_ref, lines_ref):
    scale = local_scale(got_ref, lines_ref)
    part = None
    for half, (tile_ref, plain_ref) in enumerate(((mine_ref, plain_mine_ref), (other_ref, plain_other_ref))):
        wide = jnp.concatenate(scale[half * PEERS // 2 : (half + 1) * PEERS // 2], axis=1)
        scaled = (tile_ref[...] * wide).astype(BF16)
        product = jnp.dot(scaled, plain_ref[1], preferred_element_type=F32)
        part = product if part is None else part + product
    out_ref[...] = part.reshape(PEERS, LANES, LANES).astype(BF16)


def finish_kernel(got_ref, scale_ref, out_ref):
    total = got_ref[0].astype(F32)
    for peer in range(1, PEERS):
        total += got_ref[peer].astype(F32)
    scale = scale_ref[pl.ds(lax.axis_index(SAME_ROWS), 1)]
    out_ref[...] = total * jnp.broadcast_to(scale, (LANES, LANES)).T


def call(kernel, outs, *args, scratch=(), flops=0, exps=0, limit=VMEM_LIMIT, **specs):
    moved = sum(math.prod(a.shape) * a.dtype.itemsize for a in args)
    return pl.pallas_call(
        kernel,
        out_shape=outs,
        **specs,
        scratch_shapes=scratch,
        compiler_params=pltpu.CompilerParams(vmem_limit_bytes=limit),
        cost_estimate=pl.CostEstimate(flops=flops, bytes_accessed=moved, transcendentals=exps),
    )(*args)


def near(array):
    return pltpu.with_memory_space_constraint(array, pltpu.VMEM)


def exchange(array, axes):
    return lax.all_to_all(array, axes, 0, 0)


def turned(array, axes):
    swaps = [[(place, place ^ turn) for place in range(SIDES)] for turn in range(1, SIDES)]
    return [array] + [lax.ppermute(array, axes, swap) for swap in swaps]


def on_device(feats_one, feats_two, w_first, w_second):
    short = pltpu.VMEM((PEERS, PEERS, LANES), BF16)
    wide = pltpu.VMEM((PEERS, PEERS, LANES), F32)
    lines = pltpu.VMEM((PEERS, LANES), F32)
    unit_one, plain_two = call(
        embed_kernel,
        (pltpu.VMEM((LANES, LANES), BF16), pltpu.VMEM((PEERS // 2, LANES, LANES), BF16)),
        feats_one,
        feats_two,
        w_first,
        w_second,
        in_specs=[pl.BlockSpec(memory_space=pltpu.HBM)] * 4,
        limit=60 * 2**20,
        scratch=(
            pltpu.VMEM((2 * LANES, feats_one.shape[1]), BF16),
            pltpu.VMEM(w_first.shape, BF16),
            pltpu.VMEM(w_second.shape, BF16),
            pltpu.SemaphoreType.DMA((PIECES + 3,)),
        ),
        flops=4 * LANES * w_first.shape[0] * w_first.shape[1],
    )
    mine = exchange(plain_two, RING)
    strip = jnp.stack(turned(unit_one, ALONG_X))
    half = pltpu.VMEM((SIDE, HALF), F32)
    blocks = pltpu.VMEM((PEERS, LANES, LANES), BF16)
    work = dict(flops=2 * SIDE * HALF * LANES, exps=SIDE * HALF)
    mine = call(unit_kernel, pltpu.VMEM((2, HALF, LANES), BF16), near(mine), flops=FLOPS_HINT)
    mine, *units_left = lax.optimization_barrier((mine, *turned(strip, ALONG_Y)))
    units_left = [near(part) for part in units_left]
    other = near(lax.ppermute(mine, "c", SWAP))
    mine = near(mine)
    tile_mine, left, first = call(mine_kernel, (half, blocks, lines), *units_left, mine, scratch=(blocks,), **work)
    tile_other, sums = call(other_kernel, (half, short), near(left), other, near(first), scratch=(lines,), **work)
    tile = (near(tile_mine), near(tile_other))
    for sweep in range(SWEEPS):
        if sweep:
            sums = call(rows_kernel, short, sums, *tile, scratch=(lines,))
        sums = near(exchange(sums, SAME_ROWS))
        totals = wide if sweep == SWEEPS - 1 else short
        sums, row_scale = call(cols_kernel, (totals, lines), sums, *tile, scratch=(lines,))
        sums = near(exchange(sums, SAME_COLS))
    parts = call(map_kernel, blocks, sums, *tile, mine, other, scratch=(lines,))
    parts = near(exchange(parts, SAME_ROWS))
    return call(finish_kernel, jax.ShapeDtypeStruct((LANES, LANES), F32), parts, row_scale)


def solution(mesh):
    fine = Mesh(mesh.devices.reshape((2,) * 8), AXES)
    row, col = AXES[:4], AXES[4:]
    return jax.shard_map(
        on_device,
        mesh=fine,
        in_specs=(P(row + col, None), P(col + row, None), P(), P()),
        out_specs=P(row + col, None),
        check_vma=False,
    )
```

```python
import math

import jax
import jax.numpy as jnp
from jax import lax
from jax.experimental import pallas as pl
from jax.experimental.pallas import tpu as pltpu
from jax.sharding import Mesh
from jax.sharding import PartitionSpec as P

SWEEPS = 3
PIECES = 6
FLOPS_HINT = 10**9
PEERS = 16
LANES = 128
SIDE = PEERS * LANES
EXPONENT = 20.0 * math.log2(math.e)
AXES = ("xh", "xl", "zh", "c", "yh", "yl", "zm", "zl")
SAME_ROWS = ("xh", "xl", "yh", "yl")
ALONG_X, ALONG_Y = SAME_ROWS[:2], SAME_ROWS[2:]
SIDES = 4
SAME_COLS = ("c", "zh", "zm", "zl")
RING = SAME_COLS[1:]
HALF = SIDE // 2
SWAP = [(0, 1), (1, 0)]
F32, BF16 = jnp.float32, jnp.bfloat16
VMEM_LIMIT = 16 * 2**20


def unit_of(plain):
    wide = plain.astype(F32)
    return (wide / jnp.sqrt(jnp.sum(wide * wide, axis=1, keepdims=True) + 1e-06)).astype(BF16)


def embed_kernel(one_hbm, two_hbm, first_hbm, second_hbm, unit_ref, plain_ref, feats_ref, first_ref, second_ref, sems):
    depth = first_hbm.shape[0] // PIECES
    copies = [
        pltpu.make_async_copy(one_hbm, feats_ref.at[pl.ds(0, LANES)], sems.at[PIECES]),
        pltpu.make_async_copy(two_hbm, feats_ref.at[pl.ds(LANES, LANES)], sems.at[PIECES + 1]),
    ]
    for piece in range(PIECES):
        place = pl.ds(piece * depth, depth)
        copies.append(pltpu.make_async_copy(first_hbm.at[place], first_ref.at[place], sems.at[piece]))
    copies.append(pltpu.make_async_copy(second_hbm, second_ref, sems.at[PIECES + 2]))
    for copy in copies:
        copy.start()
    copies[0].wait()
    copies[1].wait()
    hidden = None
    for piece in range(PIECES):
        copies[2 + piece].wait()
        place = slice(piece * depth, (piece + 1) * depth)
        part = jnp.dot(feats_ref[:, place], first_ref[place], preferred_element_type=F32)
        hidden = part if hidden is None else hidden + part
    hidden = jnp.maximum(hidden, 0.0).astype(BF16)
    copies[-1].wait()
    plain = jnp.dot(hidden, second_ref[...], preferred_element_type=F32).astype(BF16)
    unit_ref[...] = unit_of(plain[:LANES])
    for peer in range(plain_ref.shape[0]):
        plain_ref[peer] = plain[LANES:]


def row_totals(parts):
    return jnp.sum(parts.T, axis=0, keepdims=True)


def fill(out_ref, lines_ref):
    lines = lines_ref[...].astype(out_ref.dtype)
    for peer in range(PEERS):
        out_ref[peer] = lines


def half_tile(left_ref, rows_ref, tile_ref, lines_ref):
    for step in range(PEERS // 2):
        left = left_ref[2 * step : 2 * step + 2].reshape(2 * LANES, LANES)
        rows = slice(step * 2 * LANES, (step + 1) * 2 * LANES)
        parts = jnp.zeros((2 * LANES, LANES), F32)
        for chunk in range(PEERS // 4):
            cols = slice(chunk * 2 * LANES, (chunk + 1) * 2 * LANES)
            dots = lax.dot_general(left, rows_ref[0, cols], (((1,), (1,)), ((), ())), preferred_element_type=F32)
            block = jnp.exp2(dots * EXPONENT)
            tile_ref[rows, cols] = block
            parts += block[:, :LANES] + block[:, LANES:]
        lines_ref[2 * step : 2 * step + 1] = row_totals(parts[:LANES])
        lines_ref[2 * step + 1 : 2 * step + 2] = row_totals(parts[LANES:])


def unit_kernel(plain_ref, rows_ref):
    plain = plain_ref[...].reshape(HALF, LANES)
    rows_ref[0] = unit_of(plain)
    rows_ref[1] = plain


def mine_kernel(*refs):
    *got_refs, rows_ref, tile_ref, left_ref, lines_ref, held_ref = refs
    for turn, got_ref in enumerate(got_refs):
        held_ref[turn * SIDES : (turn + 1) * SIDES] = got_ref[...]
    along_x, along_y = lax.axis_index(ALONG_X), lax.axis_index(ALONG_Y)
    for place in range(PEERS):
        from_x, from_y = along_x ^ (place // SIDES), along_y ^ (place % SIDES)
        left_ref[place] = held_ref[from_y * SIDES + from_x]
    half_tile(left_ref, rows_ref, tile_ref, lines_ref)


def other_kernel(left_ref, rows_ref, first_ref, tile_ref, sums_ref, lines_ref):
    half_tile(left_ref, rows_ref, tile_ref, lines_ref)
    lines_ref[...] += first_ref[...]
    fill(sums_ref, lines_ref)


def core_lines():
    core = lax.axis_index("c")
    return [pl.ds(pl.multiple_of(half * (PEERS // 2), PEERS // 2), PEERS // 2) for half in (core, 1 - core)]


def scale_of(got_ref):
    total = got_ref[0].astype(F32)
    for peer in range(1, PEERS):
        total += got_ref[peer].astype(F32)
    return 1.0 / total


def cols_kernel(got_ref, mine_ref, other_ref, sums_ref, scale_ref, lines_ref):
    scale = scale_of(got_ref)
    scale_ref[...] = scale
    chunks = PEERS // 2
    parts = [jnp.zeros((8, LANES), F32) for _ in range(PEERS)]
    for block in range(PEERS):
        rows = slice(block * LANES, (block + 1) * LANES)
        factor = jnp.broadcast_to(scale[block : block + 1], (LANES, LANES)).T
        for chunk in range(PEERS):
            half_ref, at = (mine_ref, other_ref)[chunk // chunks], chunk % chunks
            product = half_ref[rows, at * LANES : (at + 1) * LANES] * factor
            parts[chunk] += jnp.sum(product.reshape(LANES // 8, 8, LANES), axis=0)
    lines = [jnp.sum(part, axis=0, keepdims=True) for part in parts]
    for half, place in enumerate(core_lines()):
        lines_ref[place] = jnp.concatenate(lines[half * chunks : (half + 1) * chunks], axis=0)
    fill(sums_ref, lines_ref)


def local_scale(got_ref, lines_ref):
    lines_ref[...] = scale_of(got_ref)
    halves = [lines_ref[place] for place in core_lines()]
    return [half[row : row + 1] for half in halves for row in range(PEERS // 2)]


def rows_kernel(got_ref, mine_ref, other_ref, sums_ref, lines_ref):
    scale = local_scale(got_ref, lines_ref)
    for block in range(PEERS):
        rows = slice(block * LANES, (block + 1) * LANES)
        parts = None
        for chunk in range(PEERS):
            half_ref, at = (mine_ref, other_ref)[2 * chunk // PEERS], chunk % (PEERS // 2)
            product = half_ref[rows, at * LANES : (at + 1) * LANES] * scale[chunk]
            parts = product if parts is None else parts + product
        lines_ref[block : block + 1] = row_totals(parts)
    fill(sums_ref, lines_ref)


def map_kernel(got_ref, mine_ref, other_ref, plain_mine_ref, plain_other_ref, out_ref, lines_ref):
    scale = local_scale(got_ref, lines_ref)
    part = None
    for half, (tile_ref, plain_ref) in enumerate(((mine_ref, plain_mine_ref), (other_ref, plain_other_ref))):
        wide = jnp.concatenate(scale[half * PEERS // 2 : (half + 1) * PEERS // 2], axis=1)
        scaled = (tile_ref[...] * wide).astype(BF16)
        product = jnp.dot(scaled, plain_ref[1], preferred_element_type=F32)
        part = product if part is None else part + product
    out_ref[...] = part.reshape(PEERS, LANES, LANES).astype(BF16)


def finish_kernel(got_ref, scale_ref, out_ref):
    total = got_ref[0].astype(F32)
    for peer in range(1, PEERS):
        total += got_ref[peer].astype(F32)
    scale = scale_ref[pl.ds(lax.axis_index(SAME_ROWS), 1)]
    out_ref[...] = total * jnp.broadcast_to(scale, (LANES, LANES)).T


def call(kernel, outs, *args, scratch=(), flops=0, exps=0, limit=VMEM_LIMIT, **specs):
    moved = sum(math.prod(a.shape) * a.dtype.itemsize for a in args)
    return pl.pallas_call(
        kernel,
        out_shape=outs,
        **specs,
        scratch_shapes=scratch,
        compiler_params=pltpu.CompilerParams(vmem_limit_bytes=limit),
        cost_estimate=pl.CostEstimate(flops=flops, bytes_accessed=moved, transcendentals=exps),
    )(*args)


def near(array):
    return pltpu.with_memory_space_constraint(array, pltpu.VMEM)


def exchange(array, axes):
    return lax.all_to_all(array, axes, 0, 0)


def turned(array, axes):
    swaps = [[(place, place ^ turn) for place in range(SIDES)] for turn in range(1, SIDES)]
    return [array] + [lax.ppermute(array, axes, swap) for swap in swaps]


def on_device(feats_one, feats_two, w_first, w_second):
    short = pltpu.VMEM((PEERS, PEERS, LANES), BF16)
    wide = pltpu.VMEM((PEERS, PEERS, LANES), F32)
    lines = pltpu.VMEM((PEERS, LANES), F32)
    unit_one, plain_two = call(
        embed_kernel,
        (pltpu.VMEM((LANES, LANES), BF16), pltpu.VMEM((PEERS // 2, LANES, LANES), BF16)),
        feats_one,
        feats_two,
        w_first,
        w_second,
        in_specs=[pl.BlockSpec(memory_space=pltpu.HBM)] * 4,
        limit=60 * 2**20,
        scratch=(
            pltpu.VMEM((2 * LANES, feats_one.shape[1]), BF16),
            pltpu.VMEM(w_first.shape, BF16),
            pltpu.VMEM(w_second.shape, BF16),
            pltpu.SemaphoreType.DMA((PIECES + 3,)),
        ),
        flops=4 * LANES * w_first.shape[0] * w_first.shape[1],
    )
    mine = exchange(plain_two, RING)
    strip = jnp.stack(turned(unit_one, ALONG_X))
    half = pltpu.VMEM((SIDE, HALF), F32)
    blocks = pltpu.VMEM((PEERS, LANES, LANES), BF16)
    work = dict(flops=2 * SIDE * HALF * LANES, exps=SIDE * HALF)
    mine = call(unit_kernel, pltpu.VMEM((2, HALF, LANES), BF16), near(mine), flops=FLOPS_HINT)
    mine, *units_left = lax.optimization_barrier((mine, *turned(strip, ALONG_Y)))
    units_left = [near(part) for part in units_left]
    other = near(lax.ppermute(mine, "c", SWAP))
    mine = near(mine)
    tile_mine, left, first = call(mine_kernel, (half, blocks, lines), *units_left, mine, scratch=(blocks,), **work)
    tile_other, sums = call(other_kernel, (half, short), near(left), other, near(first), scratch=(lines,), **work)
    tile = (near(tile_mine), near(tile_other))
    for sweep in range(SWEEPS):
        if sweep:
            sums = call(rows_kernel, short, sums, *tile, scratch=(lines,))
        sums = near(exchange(sums, ALONG_Y + ALONG_X))
        totals = wide if sweep == SWEEPS - 1 else short
        sums, row_scale = call(cols_kernel, (totals, lines), sums, *tile, scratch=(lines,))
        sums = near(exchange(sums, ("c", "zm", "zh", "zl")))
    parts = call(map_kernel, blocks, sums, *tile, mine, other, scratch=(lines,))
    parts = near(exchange(parts, SAME_ROWS))
    return call(finish_kernel, jax.ShapeDtypeStruct((LANES, LANES), F32), parts, row_scale)


def solution(mesh):
    fine = Mesh(mesh.devices.reshape((2,) * 8), AXES)
    row, col = AXES[:4], AXES[4:]
    return jax.shard_map(
        on_device,
        mesh=fine,
        in_specs=(P(row + col, None), P(col + row, None), P(), P()),
        out_specs=P(row + col, None),
        check_vma=False,
    )
```
